512 devices in a mesh: row: 64 (over y, x, z_hi), col: 8 (over z_lo, core).
Axes of the slice: x: 4, y: 8, z: 8 (z_hi: 2, z_lo: 4; z = z_hi * 4 + z_lo), core: 2. Of those that a mesh axis runs over, the one named last changes fastest.
Arguments:
- boundary_in: bfloat16 [2, 64, 8, 192, 768], P(None, 'row', 'col'), may hold values from -6 to 6
- site_tensors: bfloat16 [2, 64, 8, 2, 4, 4, 4, 4], P(None, 'row', 'col'), may hold values from -1.5 to 1.5
- spin_config: int32 [2, 64, 8], P(None, 'row', 'col'), may hold values from 0 to 1
- leg_charges: int32 [2, 64, 8, 4, 4], P(None, 'row', 'col'), may hold values from -1 to 1
- bond_charges: int32 [2, 64, 8, 192], P(None, 'row', 'col'), may hold values from -2 to 2
- left_proj: bfloat16 [2, 64, 8, 2, 192, 768], P(None, 'row', 'col'), may hold values from -0.4375 to 0.4375
- right_proj: bfloat16 [2, 64, 8, 2, 192, 768], P(None, 'row', 'col'), may hold values from -0.21875 to 0.21875
- proj_ranks: int32 [2, 64, 8, 2], P(None, 'row', 'col'), may hold values from 96 to 192
Outputs:
- boundary_out: bfloat16 [2, 64, 8, 192, 768], P(None, 'row', 'col')
The draws below stay inside these ranges and needn't reach their ends.
All inputs are finite; a program needn't handle non-finite values.
Results may differ from the reference program's by a relative error of at most 0.008.
Values may be sent and summed in bfloat16 or wider, within the bound.
No kernel may reach another device: no remote copies, remote signals or barrier semaphores. Data moves between devices by JAX's collectives and lax.ppermute only.
A program may use at most 64 MiB of HBM per device.

```python
import jax
import jax.numpy as jnp
from jax import lax

STATES = 2
D = 4
CHI = 192
NROWS = 64
NCOLS = 8


def draw_proj_ranks(key, part):
    key = jax.random.fold_in(key, 11)
    rank_key, spot_key = jax.random.split(key)
    rank_values = jax.random.randint(rank_key, (STATES, NROWS, NCOLS, 2), CHI // 2, CHI + 1)
    spot_index = jax.random.randint(spot_key, (), 0, STATES * NROWS * NCOLS * 2)
    flattened = rank_values.reshape(-1).at[spot_index].set(CHI)
    return flattened.reshape(STATES, NROWS, NCOLS, 2).astype(jnp.int32)


def plant(drawn, rng, least, top_value):
    spot = [jax.random.randint(jax.random.fold_in(rng, axis), (), 0, length) for axis, length in enumerate(drawn.shape)]
    longest = drawn.shape.index(max(drawn.shape))
    beside = spot[:longest] + [(spot[longest] + 1) % drawn.shape[longest]] + spot[longest + 1:]
    return drawn.at[tuple(spot)].set(least).at[tuple(beside)].set(top_value)


def block_levels(own_key, extent, pieces, low, high):
    factor_of, own = 1.0, jax.random.fold_in(own_key, 6)
    for dim, shards_of in pieces:
        draws = jnp.exp(jax.random.uniform(jax.random.fold_in(own, dim), (shards_of,), jnp.float32, low / len(pieces), high / len(pieces)))
        factor_of = factor_of * jnp.repeat(draws, extent[dim] // shards_of).reshape([-1 if axis == dim else 1 for axis in range(len(extent))])
    return factor_of


def scatter_about(key, extent, spread, bound, pieces=(), kind=jnp.bfloat16):
    drawn = jax.random.normal(key, extent, jnp.float32) * spread
    if len(pieces) > 0:
        drawn = block_levels(key, extent, pieces, -0.22, 0.18) * drawn
    return jnp.clip(drawn, min=-bound, max=bound).astype(kind)


def setup_inputs(seed: int = 0) -> dict:
    streams_of = jax.random.split(jax.random.key(seed), 9)
    boundary_in = scatter_about(streams_of[0], (STATES, NROWS, NCOLS, CHI, D * CHI), 1.0, 6.0, ((1, 64), (2, 8)))
    site_tensors = scatter_about(streams_of[1], (STATES, NROWS, NCOLS, 2, D, D, D, D), (D * D) ** -0.5, 1.5, ((1, 64), (2, 8)))
    spin_config = plant(jax.random.randint(streams_of[2], (STATES, NROWS, NCOLS), 0, 2), jax.random.fold_in(streams_of[2], 1), 0, 1).astype(jnp.int32)
    leg_charges = plant(jax.random.randint(streams_of[3], (STATES, NROWS, NCOLS, 4, D), -1, 2), jax.random.fold_in(streams_of[3], 1), -1, 1).astype(jnp.int32)
    bond_charges = plant(jax.random.randint(streams_of[4], (STATES, NROWS, NCOLS, CHI), -2, 3), jax.random.fold_in(streams_of[4], 1), -2, 2).astype(jnp.int32)
    left_proj = scatter_about(streams_of[5], (STATES, NROWS, NCOLS, 2, CHI, D * CHI), CHI ** -0.5, 0.4375, ((1, 64), (2, 8)))
    right_proj = scatter_about(streams_of[6], (STATES, NROWS, NCOLS, 2, CHI, D * CHI), (CHI * D) ** -0.5, 0.21875, ((1, 64), (2, 8)))
    proj_ranks = draw_proj_ranks(jax.random.fold_in(streams_of[8], 71), 0)
    return dict(boundary_in=boundary_in, site_tensors=site_tensors, spin_config=spin_config, leg_charges=leg_charges, bond_charges=bond_charges, left_proj=left_proj, right_proj=right_proj, proj_ranks=proj_ranks)


eps = 1e-06

def site_block(tensor, spin_value, leg_charge, toward_down):
    chosen = jnp.where(spin_value == 1, tensor[1], tensor[0])
    balance = spin_value + leg_charge[0][:, None, None, None] + leg_charge[2][None, None, :, None] - leg_charge[1][None, :, None, None] - leg_charge[3][None, None, None, :]
    masked = jnp.where(balance == 0, chosen, jnp.zeros_like(chosen))
    return jnp.where(toward_down, masked, jnp.transpose(masked, (0, 1, 3, 2)))

def mask_boundary(boundary, left_charge, incoming, right_charge):
    width = boundary.shape[0]
    legs = boundary.shape[1] // width
    shaped = boundary.reshape(width, legs, width)
    balance = left_charge[:, None, None] + incoming[None, :, None] - right_charge[None, None, :]
    return jnp.where(balance == 0, shaped, jnp.zeros_like(shaped))

def absorb(boundary, left_part, right_part, row_block, rank_from, rank_to):
    width = left_part.shape[0]
    legs = left_part.shape[1] // width
    positions = jnp.arange(width, dtype=jnp.int32)
    left_kept = jnp.where((positions < rank_from)[:, None], left_part, jnp.zeros_like(left_part))
    right_kept = jnp.where((positions < rank_to)[:, None], right_part, jnp.zeros_like(right_part))
    projected = jnp.dot(left_kept.reshape(width * legs, width), boundary.reshape(width, legs * width), preferred_element_type=jnp.float32)
    projected = projected.astype(jnp.bfloat16).reshape(width, legs * legs, width)
    block_matrix = jnp.transpose(row_block, (3, 1, 0, 2)).reshape(legs * legs, legs * legs)
    combined = jnp.einsum('yx,kxb->kyb', block_matrix.astype(jnp.float32), projected.astype(jnp.float32), precision=lax.Precision.HIGHEST).astype(jnp.bfloat16)
    result = jnp.dot(combined.reshape(width * legs, legs * width), jnp.transpose(right_kept), preferred_element_type=jnp.float32)
    return result.reshape(width, legs * width)

def normalize(values):
    return (values * lax.rsqrt(jnp.mean(values * values) + eps)).astype(jnp.bfloat16)

def reference(boundary_in, site_tensors, spin_config, leg_charges, bond_charges, left_proj, right_proj, proj_ranks):
    charge_left = jnp.roll(bond_charges, 1, axis=2)
    rank_left = jnp.roll(proj_ranks, 1, axis=2)
    row_ids = jnp.arange(NROWS, dtype=jnp.int32)

    def first_row(row_id):
        top_first = row_id % 2 == 0

        def single(boundary, tensor, spin_value, leg_charge, left_charge, right_charge, left_part, right_part, rank_from, rank_to):
            row_block = site_block(tensor, spin_value, leg_charge, top_first)
            incoming = jnp.where(top_first, leg_charge[2], leg_charge[3])
            cleaned = mask_boundary(boundary, left_charge, incoming, right_charge)
            return absorb(cleaned, left_part[0], right_part[0], row_block, rank_from[0], rank_to[0]).astype(jnp.bfloat16)
        return jax.vmap(jax.vmap(single))(boundary_in[:, row_id], site_tensors[:, row_id], spin_config[:, row_id], leg_charges[:, row_id], charge_left[:, row_id], bond_charges[:, row_id], left_proj[:, row_id], right_proj[:, row_id], rank_left[:, row_id], proj_ranks[:, row_id])
    halves = lax.map(first_row, row_ids)

    def second_row(row_id):
        top_first = row_id % 2 == 0
        partner = row_id + 1 - 2 * (row_id % 2)

        def single(received, tensor, spin_value, leg_charge, left_part, right_part, rank_from, rank_to):
            row_block = site_block(tensor, spin_value, leg_charge, jnp.logical_not(top_first))
            return normalize(absorb(received, left_part[1], right_part[1], row_block, rank_from[1], rank_to[1]))
        return jax.vmap(jax.vmap(single))(halves[partner], site_tensors[:, row_id], spin_config[:, row_id], leg_charges[:, row_id], left_proj[:, row_id], right_proj[:, row_id], rank_left[:, row_id], proj_ranks[:, row_id])
    finals = lax.map(second_row, row_ids)
    return jnp.moveaxis(finals, 0, 1)
```

```python
import functools

import jax
import jax.numpy as jnp
from jax import lax
from jax.experimental import pallas as pl
from jax.experimental.pallas import tpu as pltpu
from jax.sharding import PartitionSpec as P

eps = 1e-06
VMEM_BYTES = 32 * 1024 * 1024
GROUP = 16
LANES = 128


def passed_along(value, axis, steps):
    count = lax.axis_size(axis)
    pairs = [(source, (source + steps) % count) for source in range(count)]
    return lax.ppermute(value, axis, pairs)


def swapped(value, axis, distance):
    mask = 2**distance
    pairs = [(source, source ^ mask) for source in range(lax.axis_size(axis))]
    return lax.ppermute(value, axis, pairs)


def padded(width):
    return -(-width // LANES) * LANES


def pick(index, values):
    out = jnp.zeros_like(index)
    for j, value in enumerate(values):
        out = jnp.where(index == j, value, out)
    return out


def expand_block(s, legs, natural, site_ref, spin_ref, leg_ref, by_left_ref, by_right_ref, kron_ref):
    squared = legs * legs
    spin = spin_ref[0, 0, s]
    leg = [[leg_ref[s, 0, 0, j, t] for t in range(legs)] for j in range(4)]
    for l in range(legs):
        for e in range(legs):
            tile = jnp.where(spin == 1, site_ref[s, 0, 0, 1, l, e], site_ref[s, 0, 0, 0, l, e])
            tile = tile.astype(jnp.float32)
            by_left_ref[l * legs : (l + 1) * legs, e * legs : (e + 1) * legs] = tile
            by_right_ref[e * legs : (e + 1) * legs, l * legs : (l + 1) * legs] = tile
    turned = jnp.transpose(by_left_ref[...])[:squared, :squared]
    entries = jnp.where(natural, turned, by_right_ref[:squared, :squared])
    row = lax.broadcasted_iota(jnp.int32, (squared, squared), 0)
    col = lax.broadcasted_iota(jnp.int32, (squared, squared), 1)
    right, outer, left, inner = row // legs, row % legs, col // legs, col % legs
    up, down = jnp.where(natural, inner, outer), jnp.where(natural, outer, inner)
    balance = spin + pick(left, leg[0]) + pick(up, leg[2]) - pick(right, leg[1]) - pick(down, leg[3])
    entries = jnp.where(balance == 0, entries, 0.0).astype(jnp.bfloat16)
    size = squared * GROUP
    tall = lax.broadcasted_iota(jnp.int32, (size, squared), 0) // GROUP
    tall = (tall == lax.broadcasted_iota(jnp.int32, (size, squared), 1)).astype(jnp.bfloat16)
    wide = lax.broadcasted_iota(jnp.int32, (squared, size), 1) // GROUP
    wide = (wide == lax.broadcasted_iota(jnp.int32, (squared, size), 0)).astype(jnp.bfloat16)
    spread = jnp.dot(tall, entries, preferred_element_type=jnp.float32).astype(jnp.bfloat16)
    spread = jnp.dot(spread, wide, preferred_element_type=jnp.float32)
    row = lax.broadcasted_iota(jnp.int32, (size, size), 0)
    col = lax.broadcasted_iota(jnp.int32, (size, size), 1)
    kron_ref[...] = jnp.where(row % GROUP == col % GROUP, spread, 0.0).astype(jnp.bfloat16)


def stack_left(legs, width, left_ref, stack_ref):
    for l in range(legs):
        stack_ref[l * width : (l + 1) * width, :] = left_ref[:, l * width : (l + 1) * width]


def turn_right(legs, width, rank, right_ref, turned_ref):
    wide = padded(width)
    kept = lax.broadcasted_iota(jnp.int32, (width, width), 1) < rank
    for e in range(legs):
        turned = jnp.transpose(right_ref[:, e * width : (e + 1) * width])
        turned_ref[e * wide : e * wide + width, :] = jnp.where(kept, turned, jnp.zeros_like(turned))
        if wide > width:
            turned_ref[e * wide + width : (e + 1) * wide, :] = jnp.zeros((wide - width, width), jnp.bfloat16)


def absorb(legs, width, given, stack_ref, kron_ref, turned_ref, spaced_ref, proj_ref, comb_ref):
    wide = padded(width)
    for i in range(legs):
        spaced_ref[:, i * wide : i * wide + width] = given[:, i * width : (i + 1) * width]
        if wide > width:
            spaced_ref[:, i * wide + width : (i + 1) * wide] = jnp.zeros((width, wide - width), jnp.bfloat16)
    for l in range(legs):
        proj = jnp.dot(stack_ref[l * width : (l + 1) * width, :], spaced_ref[...], preferred_element_type=jnp.float32)
        proj_ref[l * width : (l + 1) * width, :] = proj.astype(jnp.bfloat16)
    for q in range(width // GROUP):
        part = jnp.concatenate(
            [
                proj_ref[l * width + q * GROUP : l * width + (q + 1) * GROUP, i * wide : (i + 1) * wide]
                for l in range(legs)
                for i in range(legs)
            ],
            axis=0,
        )
        comb = jnp.dot(kron_ref[...], part, preferred_element_type=jnp.float32).astype(jnp.bfloat16)
        for e in range(legs):
            for o in range(legs):
                place = (e * legs + o) * GROUP
                comb_ref[o * width + q * GROUP : o * width + (q + 1) * GROUP, e * wide : (e + 1) * wide] = (
                    comb[place : place + GROUP, :]
                )
    return jnp.dot(comb_ref[...], turned_ref[...], preferred_element_type=jnp.float32)


def prepare(
    s, step, legs, width, top_first,
    spin_in, leg_in, rank_in, site_in, left_in, right_in,
    stack_ref, kron_ref, turned_ref,
    spin_ref, leg_ref, rank_ref, site_ref, left_ref, right_ref, by_left_ref, by_right_ref, sems,
):
    copies = [
        pltpu.make_async_copy(source, target, sems.at[j])
        for j, (source, target) in enumerate(
            [(spin_in, spin_ref), (leg_in, leg_ref), (rank_in, rank_ref), (site_in, site_ref),
             (right_in.at[s, 0, 0, step], right_ref), (left_in.at[s, 0, 0, step], left_ref)]
        )
    ]
    for copy in copies:
        copy.start()
    for copy in copies[:4]:
        copy.wait()
    natural = top_first if step == 0 else jnp.logical_not(top_first)
    expand_block(s, legs, natural, site_ref, spin_ref, leg_ref, by_left_ref, by_right_ref, kron_ref)
    copies[4].wait()
    turn_right(legs, width, rank_ref[s, 0, 0, step], right_ref, turned_ref)
    copies[5].wait()
    stack_left(legs, width, left_ref, stack_ref)


def rows_kept(s, step, width, from_left_ref):
    rank = from_left_ref[s, 0, :, width + step : width + step + 1]
    return lax.broadcasted_iota(jnp.int32, (width, 1), 0) < rank


def is_top_first():
    return lax.rem(lax.axis_index("row"), 2) == 0


def put_half(s, legs, width, from_left_ref, result, half_ref):
    kept = rows_kept(s, 0, width, from_left_ref)
    for o in range(legs):
        part = jnp.where(kept, result[o * width : (o + 1) * width], 0.0)
        half_ref[0, :, o * width : (o + 1) * width] = part.astype(jnp.bfloat16)


def prepare_first_kernel(
    s, legs, width,
    spin_in, leg_in, rank_in, site_in, charge_in, given_in, left_in, right_in,
    stack_ref, kron_ref, turned_ref, given_ref, charge_ref, leg_out_ref,
    *scratch,
):
    *scratch, more = scratch
    fetch_given = pltpu.make_async_copy(given_in.at[s, 0, 0], given_ref, more.at[0])
    fetch_charge = pltpu.make_async_copy(charge_in, charge_ref, more.at[1])
    fetch_given.start()
    fetch_charge.start()
    prepare(
        s, 0, legs, width, is_top_first(),
        spin_in, leg_in, rank_in, site_in, left_in, right_in, stack_ref, kron_ref, turned_ref, *scratch,
    )
    leg_ref = scratch[1]
    for i in range(legs):
        incoming = jnp.where(is_top_first(), leg_ref[s, 0, 0, 2, i], leg_ref[s, 0, 0, 3, i])
        leg_out_ref[i : i + 1, :] = jnp.full((1, LANES), incoming, jnp.int32)
    fetch_given.wait()
    fetch_charge.wait()


def first_kernel(
    s, legs, width,
    from_left_ref, stack_ref, kron_ref, turned_ref, given_ref, charge_ref, incoming_ref,
    half_ref, spaced_ref, proj_ref, comb_ref,
):
    row_charge = from_left_ref[s, 0, :, :width].astype(jnp.float32)
    left_charge = jnp.transpose(jnp.broadcast_to(row_charge, (LANES, width)))[:, :1]
    right_charge = charge_ref[s, 0].astype(jnp.float32)
    wanted = [right_charge - incoming_ref[i : i + 1, :1].astype(jnp.float32) for i in range(legs)]
    given = given_ref[...]
    given = jnp.where(left_charge == jnp.concatenate(wanted, axis=1), given, jnp.zeros_like(given))
    result = absorb(legs, width, given, stack_ref, kron_ref, turned_ref, spaced_ref, proj_ref, comb_ref)
    put_half(s, legs, width, from_left_ref, result, half_ref)


def whole_first_kernel(
    s, legs, width,
    from_left_ref, _after, spin_in, leg_in, rank_in, site_in, charge_in, given_in, left_in, right_in,
    half_ref,
    stack_ref, kron_ref, turned_ref, given_ref, charge_ref, incoming_ref, spaced_ref, proj_ref, comb_ref,
    *scratch,
):
    prepare_first_kernel(
        s, legs, width,
        spin_in, leg_in, rank_in, site_in, charge_in, given_in, left_in, right_in,
        stack_ref, kron_ref, turned_ref, given_ref, charge_ref, incoming_ref, *scratch,
    )
    first_kernel(
        s, legs, width,
        from_left_ref, stack_ref, kron_ref, turned_ref, given_ref, charge_ref, incoming_ref,
        half_ref, spaced_ref, proj_ref, comb_ref,
    )


def prepare_second_kernel(
    s, legs, width, _after, spin_in, leg_in, rank_in, site_in, left_in, right_in,
    stack_ref, kron_ref, turned_ref, *scratch,
):
    prepare(
        s, 1, legs, width, is_top_first(),
        spin_in, leg_in, rank_in, site_in, left_in, right_in, stack_ref, kron_ref, turned_ref, *scratch,
    )


def second_kernel(
    s, legs, width, from_left_ref, received_ref, stack_ref, kron_ref, turned_ref, *rest,
):
    out_ref, spaced_ref, proj_ref, comb_ref, final_ref, sem = rest[-6:]
    result = absorb(
        legs, width, received_ref[0], stack_ref, kron_ref, turned_ref, spaced_ref, proj_ref, comb_ref
    )
    kept = rows_kept(s, 1, width, from_left_ref)
    parts = [jnp.where(kept, result[o * width : (o + 1) * width], 0.0) for o in range(legs)]
    total = sum(jnp.sum(part * part, axis=0, keepdims=True) for part in parts)
    mean = jnp.sum(total, axis=1, keepdims=True) * (1.0 / result.size)
    scale = lax.rsqrt(mean + eps)
    for o in range(legs):
        final_ref[:, o * width : (o + 1) * width] = (parts[o] * scale).astype(jnp.bfloat16)
    copy = pltpu.make_async_copy(final_ref, out_ref.at[s, 0, 0], sem)
    copy.start()
    copy.wait()


def local(
    boundary_in,
    site_tensors,
    spin_config,
    leg_charges,
    bond_charges,
    left_proj,
    right_proj,
    proj_ranks,
):
    states, width, legs = boundary_in.shape[0], boundary_in.shape[3], site_tensors.shape[4]
    squared, long, wide = legs * legs, legs * width, padded(width)
    size = squared * GROUP
    vmem = pl.BlockSpec(memory_space=pltpu.VMEM)
    hbm = pl.BlockSpec(memory_space=pltpu.HBM)
    bf16, i32 = jnp.bfloat16, jnp.int32

    edge = jnp.concatenate([bond_charges, proj_ranks], axis=3)
    from_left = passed_along(edge, "col", 1)

    ready_shapes = [((legs * width, width), bf16), ((size, size), bf16), ((legs * wide, width), bf16)]
    given_shapes = [((width, long), bf16), (bond_charges.shape, i32), ((8, LANES), i32)]
    prepare_scratch = [
        pltpu.SMEM((1, 1, states), i32),
        pltpu.SMEM(leg_charges.shape, i32),
        pltpu.SMEM(proj_ranks.shape, i32),
        pltpu.VMEM(site_tensors.shape, bf16),
        pltpu.VMEM((width, long), bf16),
        pltpu.VMEM((width, long), bf16),
        pltpu.VMEM((LANES, LANES), jnp.float32),
        pltpu.VMEM((LANES, LANES), jnp.float32),
        pltpu.SemaphoreType.DMA((6,)),
    ]
    absorb_scratch = [
        pltpu.VMEM((width, legs * wide), bf16),
        pltpu.VMEM((legs * width, legs * wide), bf16),
        pltpu.VMEM((legs * width, legs * wide), bf16),
    ]
    flops = 2 * (2 * width * long * long + long * long * GROUP)

    def call(kernel, s, name, out_shapes, in_specs, scratch, cost, **options):
        return pl.pallas_call(
            functools.partial(kernel, s, legs, width),
            out_shape=[jax.ShapeDtypeStruct(*shape) for shape in out_shapes],
            in_specs=in_specs,
            scratch_shapes=scratch,
            compiler_params=pltpu.CompilerParams(vmem_limit_bytes=VMEM_BYTES),
            cost_estimate=pl.CostEstimate(flops=int(flops * cost), bytes_accessed=8 * width * long, transcendentals=0),
            name=name,
            **options,
        )

    spins = jnp.transpose(spin_config, (1, 2, 0))
    spins, leg_charges, proj_ranks, site_tensors, bond_charges, boundary_in, left_proj, right_proj = (
        pltpu.with_memory_space_constraint(value, pltpu.HBM)
        for value in (spins, leg_charges, proj_ranks, site_tensors, bond_charges, boundary_in, left_proj, right_proj)
    )
    small = (spins, leg_charges, proj_ranks, site_tensors)
    half_shape = ((1, width, long), bf16)
    ready = call(
        prepare_first_kernel, 0, "prepare_first", ready_shapes + given_shapes, [hbm] * 8,
        prepare_scratch + [pltpu.SemaphoreType.DMA((2,))], 1, out_specs=[vmem] * 6,
    )(*small, bond_charges, boundary_in, left_proj, right_proj)
    (half,) = call(
        first_kernel, 0, "first_absorption", [half_shape], [vmem] * 7, absorb_scratch, 1, out_specs=[vmem]
    )(from_left, *ready)
    halves = [half]
    for s in range(1, states):
        (half,) = call(
            whole_first_kernel, s, "whole_first_absorption", [half_shape], [vmem] + [hbm] * 9,
            [pltpu.VMEM(*shape) for shape in ready_shapes + given_shapes]
            + absorb_scratch + prepare_scratch + [pltpu.SemaphoreType.DMA((2,))], 1, out_specs=[vmem],
        )(from_left, halves[-1], *small, bond_charges, boundary_in, left_proj, right_proj)
        halves.append(half)
    received = [swapped(half, "row", 0) for half in halves]
    readies = [
        call(
            prepare_second_kernel, s, "prepare_second", ready_shapes, [hbm] * 7, prepare_scratch, 1,
            out_specs=[vmem] * 3,
        )(halves[-1], *small, left_proj, right_proj)
        for s in range(states)
    ]
    out = None
    for s in range(states):
        more = [] if out is None else [out]
        (out,) = call(
            second_kernel, s, "second_absorption", [(boundary_in.shape, bf16)], [vmem] * 5 + [hbm] * len(more),
            absorb_scratch + [pltpu.VMEM((width, long), bf16), pltpu.SemaphoreType.DMA], 1,
            out_specs=[hbm], input_output_aliases={5: 0} if more else {},
        )(from_left, received[s], *readies[s], *more)
    return out


def solution(mesh):
    placed = (
        P(None, "row", "col", None, None),
        P(None, "row", "col", None, None, None, None, None),
        P(None, "row", "col"),
        P(None, "row", "col", None, None),
        P(None, "row", "col", None),
        P(None, "row", "col", None, None, None),
        P(None, "row", "col", None, None, None),
        P(None, "row", "col", None),
    )
    return jax.shard_map(
        local,
        mesh=mesh,
        in_specs=placed,
        out_specs=P(None, "row", "col", None, None),
        check_vma=False,
    )
```

```python
import functools

import jax
import jax.numpy as jnp
from jax import lax
from jax.experimental import pallas as pl
from jax.experimental.pallas import tpu as pltpu
from jax.sharding import PartitionSpec as P

eps = 1e-06
VMEM_BYTES = 32 * 1024 * 1024
GROUP = 16
LANES = 128


def passed_along(value, axis, steps):
    count = lax.axis_size(axis)
    pairs = [(source, (source + steps) % count) for source in range(count)]
    return lax.ppermute(value, axis, pairs)


def swapped(value, axis, distance):
    mask = 2**distance
    pairs = [(source, source ^ mask) for source in range(lax.axis_size(axis))]
    return lax.ppermute(value, axis, pairs)


def pick(index, values):
    out = jnp.zeros_like(index)
    for j, value in enumerate(values):
        out = jnp.where(index == j, value, out)
    return out


def expand_block(s, legs, natural, site_ref, spin_ref, leg_ref, by_left_ref, by_right_ref, kron_ref):
    squared = legs * legs
    spin = spin_ref[0, 0, s]
    leg = [[leg_ref[s, 0, 0, j, t] for t in range(legs)] for j in range(4)]
    for l in range(legs):
        for e in range(legs):
            tile = jnp.where(spin == 1, site_ref[s, 0, 0, 1, l, e], site_ref[s, 0, 0, 0, l, e])
            tile = tile.astype(jnp.float32)
            by_left_ref[l * legs : (l + 1) * legs, e * legs : (e + 1) * legs] = tile
            by_right_ref[e * legs : (e + 1) * legs, l * legs : (l + 1) * legs] = tile
    turned = jnp.transpose(by_left_ref[...])[:squared, :squared]
    entries = jnp.where(natural, turned, by_right_ref[:squared, :squared])
    row = lax.broadcasted_iota(jnp.int32, (squared, squared), 0)
    col = lax.broadcasted_iota(jnp.int32, (squared, squared), 1)
    right, outer, left, inner = row // legs, row % legs, col // legs, col % legs
    up, down = jnp.where(natural, inner, outer), jnp.where(natural, outer, inner)
    balance = spin + pick(left, leg[0]) + pick(up, leg[2]) - pick(right, leg[1]) - pick(down, leg[3])
    entries = jnp.where(balance == 0, entries, 0.0).astype(jnp.bfloat16)
    size = squared * GROUP
    tall = lax.broadcasted_iota(jnp.int32, (size, squared), 0) // GROUP
    tall = (tall == lax.broadcasted_iota(jnp.int32, (size, squared), 1)).astype(jnp.bfloat16)
    wide = lax.broadcasted_iota(jnp.int32, (squared, size), 1) // GROUP
    wide = (wide == lax.broadcasted_iota(jnp.int32, (squared, size), 0)).astype(jnp.bfloat16)
    spread = jnp.dot(tall, entries, preferred_element_type=jnp.float32).astype(jnp.bfloat16)
    spread = jnp.dot(spread, wide, preferred_element_type=jnp.float32)
    row = lax.broadcasted_iota(jnp.int32, (size, size), 0)
    col = lax.broadcasted_iota(jnp.int32, (size, size), 1)
    kron_ref[...] = jnp.where(row % GROUP == col % GROUP, spread, 0.0).astype(jnp.bfloat16)


def stack_left(legs, width, rank, left_ref, stack_ref):
    for l in range(legs):
        part = left_ref[:, l * width : (l + 1) * width]
        if rank is not None:
            kept = lax.broadcasted_iota(jnp.int32, (width, 1), 0) < rank
            part = jnp.where(kept, part, jnp.zeros_like(part))
        stack_ref[l * width : (l + 1) * width, :] = part


def parts_of(width):
    return [(first, min(LANES, width - first)) for first in range(0, width, LANES)]


def turn_right(legs, width, rank, right_ref, turned_ref):
    kept = lax.broadcasted_iota(jnp.int32, (width, width), 1) < rank
    for e in range(legs):
        turned = jnp.transpose(right_ref[:, e * width : (e + 1) * width])
        turned = jnp.where(kept, turned, jnp.zeros_like(turned))
        for p, (first, length) in enumerate(parts_of(width)):
            at = (p * legs + e) * LANES
            turned_ref[at : at + length, :] = turned[first : first + length, :]
            if length < LANES:
                turned_ref[at + length : at + LANES, :] = jnp.zeros((LANES - length, width), jnp.bfloat16)


def combine(legs, width, given_ref, stack_ref, kron_ref, proj_ref, comb_ref, comb_at):
    for l in range(legs):
        proj = jnp.dot(stack_ref[l * width : (l + 1) * width, :], given_ref[...], preferred_element_type=jnp.float32)
        proj_ref[l * width : (l + 1) * width, :] = proj.astype(jnp.bfloat16)
    pair = 2 * GROUP

    def piece(l, i, k):
        return proj_ref[l * width + k : l * width + k + GROUP, i * LANES : (i + 1) * LANES]

    for q in range(0, width, pair):
        part = jnp.concatenate(
            [
                jnp.concatenate([piece(l, i, q), piece(l, i, q + GROUP)], axis=1)
                for l in range(legs)
                for i in range(legs)
            ],
            axis=0,
        )
        comb = jnp.dot(kron_ref[...], part, preferred_element_type=jnp.float32).astype(jnp.bfloat16)
        for e in range(legs):
            for o in range(legs):
                place = (e * legs + o) * GROUP
                for h in range(2):
                    row = o * width + q + h * GROUP
                    comb_ref[row : row + GROUP, comb_at + e * LANES : comb_at + (e + 1) * LANES] = (
                        comb[place : place + GROUP, h * LANES : (h + 1) * LANES]
                    )


def space_given(legs, width, given, spaced_refs):
    for spaced_ref, (first, length) in zip(spaced_refs, parts_of(width)):
        for i in range(legs):
            spaced_ref[:, i * LANES : i * LANES + length] = given[:, i * width + first : i * width + first + length]
            if length < LANES:
                spaced_ref[:, i * LANES + length : (i + 1) * LANES] = jnp.zeros((width, LANES - length), jnp.bfloat16)


def space_part(legs, width, p, received, spaced_ref):
    length = parts_of(width)[p][1]
    for i in range(legs):
        spaced_ref[:, i * LANES : i * LANES + length] = received[:, i * length : (i + 1) * length]
        if length < LANES:
            spaced_ref[:, i * LANES + length : (i + 1) * LANES] = jnp.zeros((width, LANES - length), jnp.bfloat16)


def absorb(legs, width, spaced_refs, stack_ref, kron_ref, turned_ref, proj_ref, comb_ref):
    for p, spaced_ref in enumerate(spaced_refs):
        combine(legs, width, spaced_ref, stack_ref, kron_ref, proj_ref, comb_ref, p * legs * LANES)
    return jnp.dot(comb_ref[...], turned_ref[...], preferred_element_type=jnp.float32)


def prepare(
    states, step, legs, width, rank_left,
    spin_in, leg_in, rank_in, site_in, left_in, right_in, ready_refs,
    spin_ref, leg_ref, rank_ref, site_ref, left_ref, right_ref, by_left_ref, by_right_ref, sems,
):
    small = [
        pltpu.make_async_copy(source, target, sems.at[j])
        for j, (source, target) in enumerate(
            [(spin_in, spin_ref), (leg_in, leg_ref), (rank_in, rank_ref), (site_in, site_ref)]
        )
    ]
    large = [
        pltpu.make_async_copy(source.at[s, 0, 0, step], target.at[s], sems.at[4 + 2 * s + j])
        for s in states
        for j, (source, target) in enumerate([(right_in, right_ref), (left_in, left_ref)])
    ]
    for copy in small + large:
        copy.start()
    for copy in small:
        copy.wait()
    natural = is_top_first() if step == 0 else jnp.logical_not(is_top_first())
    for n, s in enumerate(states):
        stack_ref, kron_ref, turned_ref = ready_refs[3 * n : 3 * n + 3]
        expand_block(s, legs, natural, site_ref, spin_ref, leg_ref, by_left_ref, by_right_ref, kron_ref)
        large[2 * n].wait()
        turn_right(legs, width, rank_ref[s, 0, 0, step], right_ref.at[s], turned_ref)
        large[2 * n + 1].wait()
        stack_left(legs, width, None if rank_left is None else rank_left(s), left_ref.at[s], stack_ref)


def rank_of(s, step, width, from_left_ref):
    return from_left_ref[s, 0, :, width + step : width + step + 1]


def is_top_first():
    return lax.rem(lax.axis_index("row"), 2) == 0


def prepare_first_kernel(states, legs, width, *rest):
    spin_in, leg_in, rank_in, site_in, charge_in, given_in, left_in, right_in = rest[:8]
    given_ref, charge_ref, incoming_ref, *rest = rest[8:]
    ready_refs, scratch, more = rest[: 3 * len(states)], rest[3 * len(states) : -1], rest[-1]
    copies = [
        pltpu.make_async_copy(given_in.at[:, 0, 0], given_ref, more.at[0]),
        pltpu.make_async_copy(charge_in, charge_ref, more.at[1]),
    ]
    for copy in copies:
        copy.start()
    prepare(
        states, 0, legs, width, None,
        spin_in, leg_in, rank_in, site_in, left_in, right_in, ready_refs, *scratch,
    )
    leg_ref = scratch[1]
    for s in states:
        for i in range(legs):
            incoming = jnp.where(is_top_first(), leg_ref[s, 0, 0, 2, i], leg_ref[s, 0, 0, 3, i])
            incoming_ref[s, i : i + 1, :] = jnp.full((1, LANES), incoming, jnp.int32)
    for copy in copies:
        copy.wait()


def prepare_second_kernel(states, legs, width, from_left_ref, _after, *rest):
    prepare(
        states, 1, legs, width, lambda s: rank_of(s, 1, width, from_left_ref),
        *rest[:6], rest[6 : 6 + 3 * len(states)], *rest[6 + 3 * len(states) :],
    )


def first_kernel(states, legs, width, from_left_ref, given_ref, charge_ref, incoming_ref, *rest):
    count = len(parts_of(width))
    ready_refs, half_refs = rest[: 3 * len(states)], rest[-2 - count - len(states) : -2 - count]
    spaced_refs, (proj_ref, comb_ref) = rest[-2 - count : -2], rest[-2:]
    for n, s in enumerate(states):
        stack_ref, kron_ref, turned_ref = ready_refs[3 * n : 3 * n + 3]
        half_ref = half_refs[n]
        row_charge = from_left_ref[s, 0, :, :width].astype(jnp.float32)
        left_charge = jnp.transpose(jnp.broadcast_to(row_charge, (LANES, width)))[:, :1]
        right_charge = charge_ref[s, 0].astype(jnp.float32)
        wanted = [right_charge - incoming_ref[s, i : i + 1, :1].astype(jnp.float32) for i in range(legs)]
        given = given_ref[s]
        given = jnp.where(left_charge == jnp.concatenate(wanted, axis=1), given, jnp.zeros_like(given))
        space_given(legs, width, given, spaced_refs)
        result = absorb(legs, width, spaced_refs, stack_ref, kron_ref, turned_ref, proj_ref, comb_ref)
        kept = lax.broadcasted_iota(jnp.int32, (width, 1), 0) < rank_of(s, 0, width, from_left_ref)
        base = 0
        for first, length in parts_of(width):
            for o in range(legs):
                part = jnp.where(kept, result[o * width : (o + 1) * width, first : first + length], 0.0)
                half_ref[:, base + o * length : base + (o + 1) * length] = part.astype(jnp.bfloat16)
            base += legs * length


def second_kernel(states, each, legs, width, *rest):
    count = len(parts_of(width))
    received_refs, rest = rest[: len(states) if each else 1], rest[len(states) if each else 1 :]
    ready_refs = rest[: 3 * len(states)]
    out_ref, spaced_refs = rest[-6 - count], rest[-5 - count : -5]
    proj_ref, comb_ref, sum_ref, final_ref, sems = rest[-5:]
    copies = []
    for n, s in enumerate(states):
        stack_ref, kron_ref, turned_ref = ready_refs[3 * n : 3 * n + 3]
        received_ref = received_refs[n] if each else received_refs[0].at[n]
        base = 0
        for p, (_, length) in enumerate(parts_of(width)):
            space_part(legs, width, p, received_ref[:, base : base + legs * length], spaced_refs[p])
            base += legs * length
        for p, spaced_ref in enumerate(spaced_refs):
            combine(legs, width, spaced_ref, stack_ref, kron_ref, proj_ref, comb_ref, p * legs * LANES)
        squares = jnp.zeros((1, width), jnp.float32)
        for o in range(legs):
            rows = slice(o * width, (o + 1) * width)
            part = jnp.dot(comb_ref[rows, :], turned_ref[...], preferred_element_type=jnp.float32)
            sum_ref[rows, :] = part
            squares = squares + jnp.sum(part * part, axis=0, keepdims=True)
        mean = jnp.sum(squares, axis=1, keepdims=True) * (1.0 / (legs * width * width))
        scale = lax.rsqrt(mean + eps)
        for o in range(legs):
            part = sum_ref[o * width : (o + 1) * width, :] * scale
            final_ref[n, :, o * width : (o + 1) * width] = part.astype(jnp.bfloat16)
        copies.append(pltpu.make_async_copy(final_ref.at[n], out_ref.at[s, 0, 0], sems.at[n]))
        copies[-1].start()
    for copy in copies:
        copy.wait()


def local(
    boundary_in,
    site_tensors,
    spin_config,
    leg_charges,
    bond_charges,
    left_proj,
    right_proj,
    proj_ranks,
):
    states, width, legs = boundary_in.shape[0], boundary_in.shape[3], site_tensors.shape[4]
    every = list(range(states))
    squared, long = legs * legs, legs * width
    size = squared * GROUP
    count = len(parts_of(width))
    vmem = pl.BlockSpec(memory_space=pltpu.VMEM)
    hbm = pl.BlockSpec(memory_space=pltpu.HBM)
    bf16, i32 = jnp.bfloat16, jnp.int32

    edge = jnp.concatenate([bond_charges, proj_ranks], axis=3)
    from_left = passed_along(edge, "col", 1)

    ready_shapes = [((long, width), bf16), ((size, size), bf16), ((count * legs * LANES, width), bf16)]
    given_shapes = [((states, width, long), bf16), (bond_charges.shape, i32), ((states, 8, LANES), i32)]
    prepare_scratch = [
        pltpu.SMEM((1, 1, states), i32),
        pltpu.SMEM(leg_charges.shape, i32),
        pltpu.SMEM(proj_ranks.shape, i32),
        pltpu.VMEM(site_tensors.shape, bf16),
        pltpu.VMEM((states, width, long), bf16),
        pltpu.VMEM((states, width, long), bf16),
        pltpu.VMEM((LANES, LANES), jnp.float32),
        pltpu.VMEM((LANES, LANES), jnp.float32),
        pltpu.SemaphoreType.DMA((4 + 2 * states,)),
    ]
    absorb_scratch = [pltpu.VMEM((width, legs * LANES), bf16)] * count + [
        pltpu.VMEM((long, legs * LANES), bf16),
        pltpu.VMEM((long, count * legs * LANES), bf16),
    ]
    flops = 2 * (2 * width * long * long + long * long * GROUP)

    def call(kernel, name, out_shapes, in_specs, scratch, out_specs, **options):
        return pl.pallas_call(
            kernel,
            out_shape=[jax.ShapeDtypeStruct(*shape) for shape in out_shapes],
            in_specs=in_specs,
            out_specs=out_specs,
            scratch_shapes=scratch,
            compiler_params=pltpu.CompilerParams(vmem_limit_bytes=VMEM_BYTES),
            cost_estimate=pl.CostEstimate(flops=flops, bytes_accessed=8 * width * long, transcendentals=0),
            name=name,
            **options,
        )

    spins = jnp.transpose(spin_config, (1, 2, 0))
    spins, leg_charges, proj_ranks, site_tensors, bond_charges, boundary_in, left_proj, right_proj = (
        pltpu.with_memory_space_constraint(value, pltpu.HBM)
        for value in (spins, leg_charges, proj_ranks, site_tensors, bond_charges, boundary_in, left_proj, right_proj)
    )
    small = (spins, leg_charges, proj_ranks, site_tensors)
    bind = functools.partial
    given, charges, incoming, *ready = call(
        bind(prepare_first_kernel, every, legs, width), "prepare_first", given_shapes + ready_shapes * states,
        [hbm] * 8, prepare_scratch + [pltpu.SemaphoreType.DMA((2,))], [vmem] * (3 + 3 * states),
    )(*small, bond_charges, boundary_in, left_proj, right_proj)
    halves, last = [], None
    for group in [[s] for s in every]:
        more = [] if last is None else [last]
        halves.append(
            call(
                bind(first_kernel, group, legs, width), "first_absorption", [((width, long), bf16)] * len(group),
                [vmem] * (4 + 3 * len(group) + len(more)), absorb_scratch, [vmem] * len(group),
            )(from_left, given, charges, incoming, *ready[3 * group[0] : 3 * group[-1] + 3], *more)
        )
        last = halves[-1][-1]
    received = [swapped(half, "row", 0) for group in halves for half in group]
    ready = call(
        bind(prepare_second_kernel, every, legs, width), "prepare_second", ready_shapes * states,
        [vmem] * 2 + [hbm] * 6, prepare_scratch, [vmem] * (3 * states),
    )(from_left, last, *small, left_proj, right_proj)
    out = None
    for group in [[s] for s in every]:
        more = [] if out is None else [out]
        (out,) = call(
            bind(second_kernel, group, True, legs, width), "second_absorption", [(boundary_in.shape, bf16)],
            [vmem] * (4 * len(group)) + [hbm] * len(more),
            absorb_scratch
            + [
                pltpu.VMEM((long, width), jnp.float32),
                pltpu.VMEM((len(group), width, long), bf16),
                pltpu.SemaphoreType.DMA((len(group),)),
            ],
            [hbm], input_output_aliases={4 * len(group): 0} if more else {},
        )(*[received[s] for s in group], *ready[3 * group[0] : 3 * group[-1] + 3], *more)
    return out


def solution(mesh):
    placed = (
        P(None, "row", "col", None, None),
        P(None, "row", "col", None, None, None, None, None),
        P(None, "row", "col"),
        P(None, "row", "col", None, None),
        P(None, "row", "col", None),
        P(None, "row", "col", None, None, None),
        P(None, "row", "col", None, None, None),
        P(None, "row", "col", None),
    )
    return jax.shard_map(
        local,
        mesh=mesh,
        in_specs=placed,
        out_specs=P(None, "row", "col", None, None),
        check_vma=False,
    )
```

```python
import functools

import jax
import jax.numpy as jnp
from jax import lax
from jax.experimental import pallas as pl
from jax.experimental.pallas import tpu as pltpu
from jax.sharding import PartitionSpec as P

eps = 1e-06
VMEM_BYTES = 32 * 1024 * 1024
GROUP = 16
LANES = 128


def passed_along(value, axis, steps):
    count = lax.axis_size(axis)
    pairs = [(source, (source + steps) % count) for source in range(count)]
    return lax.ppermute(value, axis, pairs)


def swapped(value, axis, distance):
    mask = 2**distance
    pairs = [(source, source ^ mask) for source in range(lax.axis_size(axis))]
    return lax.ppermute(value, axis, pairs)


def pick(index, values):
    out = jnp.zeros_like(index)
    for j, value in enumerate(values):
        out = jnp.where(index == j, value, out)
    return out


def expand_block(s, legs, natural, site_ref, spin_ref, leg_ref, by_left_ref, by_right_ref, kron_ref):
    squared = legs * legs
    spin = spin_ref[0, 0, s]
    leg = [[leg_ref[s, 0, 0, j, t] for t in range(legs)] for j in range(4)]
    for l in range(legs):
        for e in range(legs):
            tile = jnp.where(spin == 1, site_ref[s, 0, 0, 1, l, e], site_ref[s, 0, 0, 0, l, e])
            tile = tile.astype(jnp.float32)
            by_left_ref[l * legs : (l + 1) * legs, e * legs : (e + 1) * legs] = tile
            by_right_ref[e * legs : (e + 1) * legs, l * legs : (l + 1) * legs] = tile
    turned = jnp.transpose(by_left_ref[...])[:squared, :squared]
    entries = jnp.where(natural, turned, by_right_ref[:squared, :squared])
    row = lax.broadcasted_iota(jnp.int32, (squared, squared), 0)
    col = lax.broadcasted_iota(jnp.int32, (squared, squared), 1)
    right, outer, left, inner = row // legs, row % legs, col // legs, col % legs
    up, down = jnp.where(natural, inner, outer), jnp.where(natural, outer, inner)
    balance = spin + pick(left, leg[0]) + pick(up, leg[2]) - pick(right, leg[1]) - pick(down, leg[3])
    entries = jnp.where(balance == 0, entries, 0.0).astype(jnp.bfloat16)
    size = squared * GROUP
    tall = lax.broadcasted_iota(jnp.int32, (size, squared), 0) // GROUP
    tall = (tall == lax.broadcasted_iota(jnp.int32, (size, squared), 1)).astype(jnp.bfloat16)
    wide = lax.broadcasted_iota(jnp.int32, (squared, size), 1) // GROUP
    wide = (wide == lax.broadcasted_iota(jnp.int32, (squared, size), 0)).astype(jnp.bfloat16)
    spread = jnp.dot(tall, entries, preferred_element_type=jnp.float32).astype(jnp.bfloat16)
    spread = jnp.dot(spread, wide, preferred_element_type=jnp.float32)
    row = lax.broadcasted_iota(jnp.int32, (size, size), 0)
    col = lax.broadcasted_iota(jnp.int32, (size, size), 1)
    kron_ref[...] = jnp.where(row % GROUP == col % GROUP, spread, 0.0).astype(jnp.bfloat16)


def stack_left(legs, width, rank, left_ref, stack_ref):
    for l in range(legs):
        part = left_ref[:, l * width : (l + 1) * width]
        if rank is not None:
            kept = lax.broadcasted_iota(jnp.int32, (width, 1), 0) < rank
            part = jnp.where(kept, part, jnp.zeros_like(part))
        stack_ref[l * width : (l + 1) * width, :] = part


def parts_of(width):
    return [(first, min(LANES, width - first)) for first in range(0, width, LANES)]


def turn_right(legs, width, rank, right_ref, turned_ref):
    kept = lax.broadcasted_iota(jnp.int32, (width, width), 1) < rank
    for e in range(legs):
        turned = jnp.transpose(right_ref[:, e * width : (e + 1) * width])
        turned = jnp.where(kept, turned, jnp.zeros_like(turned))
        for first, length in parts_of(width):
            at = legs * first + e * length
            turned_ref[at : at + length, :] = turned[first : first + length, :]


def project(legs, width, given, stack_ref, proj_ref):
    for l in range(legs):
        rows = slice(l * width, (l + 1) * width)
        proj = jnp.dot(stack_ref[rows, :], given, preferred_element_type=jnp.float32)
        proj_ref[rows, :] = proj.astype(jnp.bfloat16)


def combine(legs, width, length, kron_ref, proj_ref, comb_ref):
    side = 2 * LANES // length
    for q in range(0, width, side * GROUP):
        places = [q + h * GROUP for h in range(side)]
        part = jnp.concatenate(
            [
                jnp.concatenate(
                    [
                        proj_ref[l * width + k : l * width + k + GROUP, i * length : (i + 1) * length]
                        for k in places
                    ],
                    axis=1,
                )
                for l in range(legs)
                for i in range(legs)
            ],
            axis=0,
        )
        comb = jnp.dot(kron_ref[...], part, preferred_element_type=jnp.float32).astype(jnp.bfloat16)
        for o in range(legs):
            for h, k in enumerate(places):
                comb_ref[o * width + k : o * width + k + GROUP, :] = jnp.concatenate(
                    [
                        comb[(e * legs + o) * GROUP : (e * legs + o + 1) * GROUP, h * length : (h + 1) * length]
                        for e in range(legs)
                    ],
                    axis=1,
                )


def absorb(legs, width, givens, stack_ref, kron_ref, turned_ref, proj_refs, comb_refs):
    parts = parts_of(width)
    for given, proj_ref in zip(givens, proj_refs):
        project(legs, width, given, stack_ref, proj_ref)
    for (_, length), proj_ref, comb_ref in zip(parts, proj_refs, comb_refs):
        combine(legs, width, length, kron_ref, proj_ref, comb_ref)
    results = []
    for o in range(legs):
        result = None
        for (first, length), comb_ref in zip(parts, comb_refs):
            term = jnp.dot(
                comb_ref[o * width : (o + 1) * width, :],
                turned_ref[legs * first : legs * (first + length), :],
                preferred_element_type=jnp.float32,
            )
            result = term if result is None else result + term
        results.append(result)
    return results


def prepare(
    states, step, legs, width, rank_left,
    spin_in, leg_in, rank_in, site_in, left_in, right_in, ready_refs,
    spin_ref, leg_ref, rank_ref, site_ref, left_ref, right_ref, by_left_ref, by_right_ref, sems,
):
    small = [
        pltpu.make_async_copy(source, target, sems.at[j])
        for j, (source, target) in enumerate(
            [(spin_in, spin_ref), (leg_in, leg_ref), (rank_in, rank_ref), (site_in, site_ref)]
        )
    ]
    large = [
        pltpu.make_async_copy(source.at[s, 0, 0, step], target.at[s], sems.at[4 + 2 * s + j])
        for s in states
        for j, (source, target) in enumerate([(right_in, right_ref), (left_in, left_ref)])
    ]
    for copy in small + large:
        copy.start()
    for copy in small + large:
        copy.wait()
    natural = is_top_first() if step == 0 else jnp.logical_not(is_top_first())
    for n, s in enumerate(states):
        stack_ref, kron_ref, turned_ref = ready_refs[3 * n : 3 * n + 3]
        expand_block(s, legs, natural, site_ref, spin_ref, leg_ref, by_left_ref, by_right_ref, kron_ref)
        turn_right(legs, width, rank_ref[s, 0, 0, step], right_ref.at[s], turned_ref)
        stack_left(legs, width, None if rank_left is None else rank_left(s), left_ref.at[s], stack_ref)


def rank_of(s, step, width, from_left_ref):
    return from_left_ref[s, 0, :, width + step : width + step + 1]


def is_top_first():
    return lax.rem(lax.axis_index("row"), 2) == 0


def prepare_first_kernel(states, legs, width, *rest):
    spin_in, leg_in, rank_in, site_in, charge_in, given_in, left_in, right_in = rest[:8]
    given_ref, charge_ref, incoming_ref, *rest = rest[8:]
    ready_refs, scratch, more = rest[: 3 * len(states)], rest[3 * len(states) : -1], rest[-1]
    copies = [
        pltpu.make_async_copy(given_in.at[:, 0, 0], given_ref, more.at[0]),
        pltpu.make_async_copy(charge_in, charge_ref, more.at[1]),
    ]
    for copy in copies:
        copy.start()
    prepare(
        states, 0, legs, width, None,
        spin_in, leg_in, rank_in, site_in, left_in, right_in, ready_refs, *scratch,
    )
    leg_ref = scratch[1]
    for s in states:
        for i in range(legs):
            incoming = jnp.where(is_top_first(), leg_ref[s, 0, 0, 2, i], leg_ref[s, 0, 0, 3, i])
            incoming_ref[s, i : i + 1, :] = jnp.full((1, LANES), incoming, jnp.int32)
    for copy in copies:
        copy.wait()


def prepare_second_kernel(states, legs, width, from_left_ref, _after, *rest):
    prepare(
        states, 1, legs, width, lambda s: rank_of(s, 1, width, from_left_ref),
        *rest[:6], rest[6 : 6 + 3 * len(states)], *rest[6 + 3 * len(states) :],
    )


def first_kernel(states, legs, width, from_left_ref, given_ref, charge_ref, incoming_ref, *rest):
    parts = parts_of(width)
    count = len(parts)
    ready_refs, half_refs = rest[: 3 * len(states)], rest[-3 * count - len(states) : -3 * count]
    given_refs, proj_refs, comb_refs = rest[-3 * count : -2 * count], rest[-2 * count : -count], rest[-count:]
    for n, s in enumerate(states):
        row_charge = from_left_ref[s, 0, :, :width].astype(jnp.float32)
        left_charge = jnp.transpose(jnp.broadcast_to(row_charge, (LANES, width)))[:, :1]
        right_charge = charge_ref[s, 0].astype(jnp.float32)
        wanted = [right_charge - incoming_ref[s, i : i + 1, :1].astype(jnp.float32) for i in range(legs)]
        given = given_ref[s]
        given = jnp.where(left_charge == jnp.concatenate(wanted, axis=1), given, jnp.zeros_like(given))
        for part_ref, (first, length) in zip(given_refs, parts):
            for i in range(legs):
                at = i * width + first
                part_ref[:, i * length : (i + 1) * length] = given[:, at : at + length]
        givens = [part_ref[...] for part_ref in given_refs]
        results = absorb(legs, width, givens, *ready_refs[3 * n : 3 * n + 3], proj_refs, comb_refs)
        kept = lax.broadcasted_iota(jnp.int32, (width, 1), 0) < rank_of(s, 0, width, from_left_ref)
        for first, length in parts:
            for o, result in enumerate(results):
                part = jnp.where(kept, result[:, first : first + length], 0.0)
                at = legs * first + o * length
                half_refs[n][:, at : at + length] = part.astype(jnp.bfloat16)


def second_kernel(states, legs, width, *rest):
    parts = parts_of(width)
    count = len(parts)
    received_refs, ready_refs = rest[: len(states)], rest[len(states) : 4 * len(states)]
    proj_refs, comb_refs = rest[-3 - 2 * count : -3 - count], rest[-3 - count : -3]
    out_ref, (sum_ref, final_ref, sems) = rest[-4 - 2 * count], rest[-3:]
    copies = []
    for n, s in enumerate(states):
        givens = [received_refs[n][:, legs * first : legs * (first + length)] for first, length in parts]
        results = absorb(legs, width, givens, *ready_refs[3 * n : 3 * n + 3], proj_refs, comb_refs)
        squares = jnp.zeros((1, width), jnp.float32)
        for o, result in enumerate(results):
            sum_ref[o] = result
            squares = squares + jnp.sum(result * result, axis=0, keepdims=True)
        mean = jnp.sum(squares, axis=1, keepdims=True) * (1.0 / (legs * width * width))
        scale = lax.rsqrt(mean + eps)
        for o in range(legs):
            final_ref[n, :, o * width : (o + 1) * width] = (sum_ref[o] * scale).astype(jnp.bfloat16)
        copies.append(pltpu.make_async_copy(final_ref.at[n], out_ref.at[s, 0, 0], sems.at[n]))
        copies[-1].start()
    for copy in copies:
        copy.wait()


def local(
    boundary_in,
    site_tensors,
    spin_config,
    leg_charges,
    bond_charges,
    left_proj,
    right_proj,
    proj_ranks,
):
    states, width, legs = boundary_in.shape[0], boundary_in.shape[3], site_tensors.shape[4]
    every = list(range(states))
    squared, long = legs * legs, legs * width
    size = squared * GROUP
    vmem = pl.BlockSpec(memory_space=pltpu.VMEM)
    hbm = pl.BlockSpec(memory_space=pltpu.HBM)
    bf16, i32 = jnp.bfloat16, jnp.int32

    edge = jnp.concatenate([bond_charges, proj_ranks], axis=3)
    from_left = passed_along(edge, "col", 1)

    ready_shapes = [((long, width), bf16), ((size, size), bf16), ((long, width), bf16)]
    given_shapes = [((states, width, long), bf16), (bond_charges.shape, i32), ((states, 8, LANES), i32)]
    prepare_scratch = [
        pltpu.SMEM((1, 1, states), i32),
        pltpu.SMEM(leg_charges.shape, i32),
        pltpu.SMEM(proj_ranks.shape, i32),
        pltpu.VMEM(site_tensors.shape, bf16),
        pltpu.VMEM((states, width, long), bf16),
        pltpu.VMEM((states, width, long), bf16),
        pltpu.VMEM((LANES, LANES), jnp.float32),
        pltpu.VMEM((LANES, LANES), jnp.float32),
        pltpu.SemaphoreType.DMA((4 + 2 * states,)),
    ]
    given_scratch = [pltpu.VMEM((width, legs * length), bf16) for _, length in parts_of(width)]
    absorb_scratch = [pltpu.VMEM((long, legs * length), bf16) for _, length in parts_of(width)] * 2
    flops = 2 * (2 * width * long * long + long * long * GROUP)

    def call(kernel, name, out_shapes, in_specs, scratch, out_specs, **options):
        return pl.pallas_call(
            kernel,
            out_shape=[jax.ShapeDtypeStruct(*shape) for shape in out_shapes],
            in_specs=in_specs,
            out_specs=out_specs,
            scratch_shapes=scratch,
            compiler_params=pltpu.CompilerParams(vmem_limit_bytes=VMEM_BYTES),
            cost_estimate=pl.CostEstimate(flops=flops, bytes_accessed=8 * width * long, transcendentals=0),
            name=name,
            **options,
        )

    spins = jnp.transpose(spin_config, (1, 2, 0))
    spins, leg_charges, proj_ranks, site_tensors, bond_charges, boundary_in, left_proj, right_proj = (
        pltpu.with_memory_space_constraint(value, pltpu.HBM)
        for value in (spins, leg_charges, proj_ranks, site_tensors, bond_charges, boundary_in, left_proj, right_proj)
    )
    small = (spins, leg_charges, proj_ranks, site_tensors)
    bind = functools.partial
    given, charges, incoming, *ready = call(
        bind(prepare_first_kernel, every, legs, width), "prepare_first", given_shapes + ready_shapes * states,
        [hbm] * 8, prepare_scratch + [pltpu.SemaphoreType.DMA((2,))], [vmem] * (3 + 3 * states),
    )(*small, bond_charges, boundary_in, left_proj, right_proj)
    halves, last = [], None
    for group in [[s] for s in every]:
        more = [] if last is None else [last]
        halves.append(
            call(
                bind(first_kernel, group, legs, width), "first_absorption", [((width, long), bf16)] * len(group),
                [vmem] * (4 + 3 * len(group) + len(more)), given_scratch + absorb_scratch, [vmem] * len(group),
            )(from_left, given, charges, incoming, *ready[3 * group[0] : 3 * group[-1] + 3], *more)
        )
        last = halves[-1][-1]
    received = [swapped(half, "row", 0) for group in halves for half in group]
    ready = call(
        bind(prepare_second_kernel, every, legs, width), "prepare_second", ready_shapes * states,
        [vmem] * 2 + [hbm] * 6, prepare_scratch, [vmem] * (3 * states),
    )(from_left, last, *small, left_proj, right_proj)
    out = None
    for group in [[s] for s in every]:
        more = [] if out is None else [out]
        (out,) = call(
            bind(second_kernel, group, legs, width), "second_absorption", [(boundary_in.shape, bf16)],
            [vmem] * (4 * len(group)) + [hbm] * len(more),
            absorb_scratch
            + [
                pltpu.VMEM((legs, width, width), jnp.float32),
                pltpu.VMEM((len(group), width, long), bf16),
                pltpu.SemaphoreType.DMA((len(group),)),
            ],
            [hbm], input_output_aliases={4 * len(group): 0} if more else {},
        )(*[received[s] for s in group], *ready[3 * group[0] : 3 * group[-1] + 3], *more)
    return out


def solution(mesh):
    placed = (
        P(None, "row", "col", None, None),
        P(None, "row", "col", None, None, None, None, None),
        P(None, "row", "col"),
        P(None, "row", "col", None, None),
        P(None, "row", "col", None),
        P(None, "row", "col", None, None, None),
        P(None, "row", "col", None, None, None),
        P(None, "row", "col", None),
    )
    return jax.shard_map(
        local,
        mesh=mesh,
        in_specs=placed,
        out_specs=P(None, "row", "col", None, None),
        check_vma=False,
    )
```

```python
import functools

import jax
import jax.numpy as jnp
from jax import lax
from jax.experimental import pallas as pl
from jax.experimental.pallas import tpu as pltpu
from jax.sharding import PartitionSpec as P

eps = 1e-06
VMEM_BYTES = 32 * 1024 * 1024
GROUP = 16
LANES = 128


def passed_along(value, axis, steps):
    count = lax.axis_size(axis)
    pairs = [(source, (source + steps) % count) for source in range(count)]
    return lax.ppermute(value, axis, pairs)


def swapped(value, axis, distance):
    mask = 2**distance
    pairs = [(source, source ^ mask) for source in range(lax.axis_size(axis))]
    return lax.ppermute(value, axis, pairs)


def pick(index, values):
    out = jnp.zeros_like(index)
    for j, value in enumerate(values):
        out = jnp.where(index == j, value, out)
    return out


def expand_block(s, legs, natural, site_ref, spin_ref, leg_ref, by_left_ref, by_right_ref, kron_ref):
    squared = legs * legs
    spin = spin_ref[0, 0, s]
    leg = [[leg_ref[s, 0, 0, j, t] for t in range(legs)] for j in range(4)]
    for l in range(legs):
        for e in range(legs):
            tile = jnp.where(spin == 1, site_ref[s, 0, 0, 1, l, e], site_ref[s, 0, 0, 0, l, e])
            tile = tile.astype(jnp.float32)
            by_left_ref[l * legs : (l + 1) * legs, e * legs : (e + 1) * legs] = tile
            by_right_ref[e * legs : (e + 1) * legs, l * legs : (l + 1) * legs] = tile
    turned = jnp.transpose(by_left_ref[...])[:squared, :squared]
    entries = jnp.where(natural, turned, by_right_ref[:squared, :squared])
    row = lax.broadcasted_iota(jnp.int32, (squared, squared), 0)
    col = lax.broadcasted_iota(jnp.int32, (squared, squared), 1)
    right, outer, left, inner = row // legs, row % legs, col // legs, col % legs
    up, down = jnp.where(natural, inner, outer), jnp.where(natural, outer, inner)
    balance = spin + pick(left, leg[0]) + pick(up, leg[2]) - pick(right, leg[1]) - pick(down, leg[3])
    entries = jnp.where(balance == 0, entries, 0.0).astype(jnp.bfloat16)
    size = squared * GROUP
    tall = lax.broadcasted_iota(jnp.int32, (size, squared), 0) // GROUP
    tall = (tall == lax.broadcasted_iota(jnp.int32, (size, squared), 1)).astype(jnp.bfloat16)
    wide = lax.broadcasted_iota(jnp.int32, (squared, size), 1) // GROUP
    wide = (wide == lax.broadcasted_iota(jnp.int32, (squared, size), 0)).astype(jnp.bfloat16)
    spread = jnp.dot(tall, entries, preferred_element_type=jnp.float32).astype(jnp.bfloat16)
    spread = jnp.dot(spread, wide, preferred_element_type=jnp.float32)
    row = lax.broadcasted_iota(jnp.int32, (size, size), 0)
    col = lax.broadcasted_iota(jnp.int32, (size, size), 1)
    kron_ref[...] = jnp.where(row % GROUP == col % GROUP, spread, 0.0).astype(jnp.bfloat16)


def stack_left(legs, width, rank, left_ref, stack_ref):
    for l in range(legs):
        part = left_ref[:, l * width : (l + 1) * width]
        if rank is not None:
            kept = lax.broadcasted_iota(jnp.int32, (width, 1), 0) < rank
            part = jnp.where(kept, part, jnp.zeros_like(part))
        stack_ref[l * width : (l + 1) * width, :] = part


def parts_of(width):
    return [(first, min(LANES, width - first)) for first in range(0, width, LANES)]


def turn_right(legs, width, rank, right_ref, turned_ref):
    kept = lax.broadcasted_iota(jnp.int32, (width, width), 1) < rank
    for e in range(legs):
        turned = jnp.transpose(right_ref[:, e * width : (e + 1) * width])
        turned = jnp.where(kept, turned, jnp.zeros_like(turned))
        for first, length in parts_of(width):
            at = legs * first + e * length
            turned_ref[at : at + length, :] = turned[first : first + length, :]


def project(legs, width, given, stack_ref, proj_ref):
    for l in range(legs):
        rows = slice(l * width, (l + 1) * width)
        proj = jnp.dot(stack_ref[rows, :], given, preferred_element_type=jnp.float32)
        proj_ref[rows, :] = proj.astype(jnp.bfloat16)


def combine(legs, width, length, kron_ref, proj_ref, comb_ref):
    side = 2 * LANES // length
    for q in range(0, width, side * GROUP):
        places = [q + h * GROUP for h in range(side)]
        part = jnp.concatenate(
            [
                jnp.concatenate(
                    [
                        proj_ref[l * width + k : l * width + k + GROUP, i * length : (i + 1) * length]
                        for k in places
                    ],
                    axis=1,
                )
                for l in range(legs)
                for i in range(legs)
            ],
            axis=0,
        )
        comb = jnp.dot(kron_ref[...], part, preferred_element_type=jnp.float32).astype(jnp.bfloat16)
        for o in range(legs):
            for h, k in enumerate(places):
                comb_ref[o * width + k : o * width + k + GROUP, :] = jnp.concatenate(
                    [
                        comb[(e * legs + o) * GROUP : (e * legs + o + 1) * GROUP, h * length : (h + 1) * length]
                        for e in range(legs)
                    ],
                    axis=1,
                )


def absorb(legs, width, givens, stack_ref, kron_ref, turned_ref, proj_refs, comb_refs):
    parts = parts_of(width)
    for given, proj_ref in zip(givens, proj_refs):
        project(legs, width, given, stack_ref, proj_ref)
    for (_, length), proj_ref, comb_ref in zip(parts, proj_refs, comb_refs):
        combine(legs, width, length, kron_ref, proj_ref, comb_ref)
    results = []
    for o in range(legs):
        result = None
        for (first, length), comb_ref in zip(parts, comb_refs):
            term = jnp.dot(
                comb_ref[o * width : (o + 1) * width, :],
                turned_ref[legs * first : legs * (first + length), :],
                preferred_element_type=jnp.float32,
            )
            result = term if result is None else result + term
        results.append(result)
    return results


def prepare(
    states, step, legs, width, natural, rank_left, fetch_small,
    spin_in, leg_in, rank_in, site_in, left_in, right_in, ready_refs,
    spin_ref, leg_ref, rank_ref, site_ref, left_ref, right_ref, by_left_ref, by_right_ref, sems,
):
    copies = [
        pltpu.make_async_copy(source.at[s, 0, 0, step], target.at[s], sems.at[4 + 2 * s + j])
        for s in states
        for j, (source, target) in enumerate([(right_in, right_ref), (left_in, left_ref)])
    ]
    if fetch_small:
        copies += [
            pltpu.make_async_copy(source, target, sems.at[j])
            for j, (source, target) in enumerate(
                [(spin_in, spin_ref), (leg_in, leg_ref), (rank_in, rank_ref), (site_in, site_ref)]
            )
        ]
    for copy in copies:
        copy.start()
    for copy in copies:
        copy.wait()
    for n, s in enumerate(states):
        stack_ref, kron_ref, turned_ref = ready_refs[3 * n : 3 * n + 3]
        expand_block(s, legs, natural, site_ref, spin_ref, leg_ref, by_left_ref, by_right_ref, kron_ref)
        turn_right(legs, width, rank_ref[s, 0, 0, step], right_ref.at[s], turned_ref)
        stack_left(legs, width, None if rank_left is None else rank_left(s), left_ref.at[s], stack_ref)


def rank_of(s, step, width, from_left_ref):
    return from_left_ref[s, 0, :, width + step : width + step + 1]


def is_top_first():
    return lax.rem(lax.axis_index("row"), 2) == 0


def prepare_first_kernel(states, legs, width, *rest):
    spin_in, leg_in, rank_in, site_in, charge_in, given_in, left_in, right_in = rest[:8]
    given_ref, charge_ref, incoming_ref, *rest = rest[8:]
    ready_refs, scratch, more = rest[: 3 * len(states)], rest[3 * len(states) : -1], rest[-1]
    sources = (spin_in, leg_in, rank_in, site_in, left_in, right_in)
    top_first = is_top_first()
    copies = [
        pltpu.make_async_copy(given_in.at[0, 0, 0], given_ref.at[0], more.at[0]),
        pltpu.make_async_copy(charge_in, charge_ref, more.at[1]),
    ]
    for copy in copies:
        copy.start()
    prepare(states[:1], 0, legs, width, top_first, None, True, *sources, ready_refs[:3], *scratch)
    leg_ref = scratch[1]
    for s in states:
        for i in range(legs):
            incoming = jnp.where(top_first, leg_ref[s, 0, 0, 2, i], leg_ref[s, 0, 0, 3, i])
            incoming_ref[s, i : i + 1, :] = jnp.full((1, LANES), incoming, jnp.int32)
    for copy in copies:
        copy.wait()

    @pl.when(top_first)
    def _():
        fetches = [pltpu.make_async_copy(given_in.at[s, 0, 0], given_ref.at[s], more.at[s + 1]) for s in states[1:]]
        for fetch in fetches:
            fetch.start()
        prepare(states[1:], 0, legs, width, top_first, None, False, *sources, ready_refs[3:], *scratch)
        for fetch in fetches:
            fetch.wait()


def prepare_second_kernel(states, legs, width, from_left_ref, _after, *rest):
    prepare(
        states, 1, legs, width, jnp.logical_not(is_top_first()), lambda s: rank_of(s, 1, width, from_left_ref), True,
        *rest[:6], rest[6 : 6 + 3 * len(states)], *rest[6 + 3 * len(states) :],
    )


def absorb_first(
    s, legs, width, from_left_ref, given_ref, charge_ref, incoming_ref, ready_refs, half_ref, scratch
):
    parts = parts_of(width)
    count = len(parts)
    given_refs, proj_refs, comb_refs = scratch[:count], scratch[count : 2 * count], scratch[2 * count :]
    row_charge = from_left_ref[s, 0, :, :width].astype(jnp.float32)
    left_charge = jnp.transpose(jnp.broadcast_to(row_charge, (LANES, width)))[:, :1]
    right_charge = charge_ref[s, 0].astype(jnp.float32)
    wanted = [right_charge - incoming_ref[s, i : i + 1, :1].astype(jnp.float32) for i in range(legs)]
    given = given_ref[s]
    given = jnp.where(left_charge == jnp.concatenate(wanted, axis=1), given, jnp.zeros_like(given))
    for part_ref, (first, length) in zip(given_refs, parts):
        for i in range(legs):
            at = i * width + first
            part_ref[:, i * length : (i + 1) * length] = given[:, at : at + length]
    givens = [part_ref[...] for part_ref in given_refs]
    results = absorb(legs, width, givens, *ready_refs, proj_refs, comb_refs)
    kept = lax.broadcasted_iota(jnp.int32, (width, 1), 0) < rank_of(s, 0, width, from_left_ref)
    for first, length in parts:
        for o, result in enumerate(results):
            part = jnp.where(kept, result[:, first : first + length], 0.0)
            at = legs * first + o * length
            half_ref[:, at : at + length] = part.astype(jnp.bfloat16)


def first_kernel(states, legs, width, from_left_ref, given_ref, charge_ref, incoming_ref, *rest):
    count = len(states)
    ready_refs, half_refs, scratch = rest[: 3 * count], rest[3 * count : 4 * count], rest[4 * count :]
    edges = (from_left_ref, given_ref, charge_ref, incoming_ref)
    absorb_first(0, legs, width, *edges, ready_refs[:3], half_refs[0], scratch)

    @pl.when(is_top_first())
    def _():
        for s in states[1:]:
            absorb_first(s, legs, width, *edges, ready_refs[3 * s : 3 * s + 3], half_refs[s], scratch)


def rest_kernel(s, legs, width, from_left_ref, charge_ref, incoming_ref, half_in_ref, _after, *rest):
    spin_in, leg_in, rank_in, site_in, given_in, left_in, right_in, half_ref, given_ref = rest[:9]
    ready_refs, sem, rest = rest[9:12], rest[12], rest[13:]
    scratch, more = rest[: 3 * len(parts_of(width))], rest[3 * len(parts_of(width)) :]
    top_first = is_top_first()

    @pl.when(top_first)
    def _():
        half_ref[...] = half_in_ref[...]

    @pl.when(jnp.logical_not(top_first))
    def _():
        fetch = pltpu.make_async_copy(given_in.at[s, 0, 0], given_ref.at[s], sem)
        fetch.start()
        prepare(
            [s], 0, legs, width, top_first, None, True,
            spin_in, leg_in, rank_in, site_in, left_in, right_in, ready_refs, *more,
        )
        fetch.wait()
        absorb_first(
            s, legs, width, from_left_ref, given_ref, charge_ref, incoming_ref, ready_refs, half_ref, scratch
        )


def second_kernel(states, legs, width, *rest):
    parts = parts_of(width)
    count = len(parts)
    received_refs, ready_refs = rest[: len(states)], rest[len(states) : 4 * len(states)]
    proj_refs, comb_refs = rest[-3 - 2 * count : -3 - count], rest[-3 - count : -3]
    out_ref, (sum_ref, final_ref, sems) = rest[-4 - 2 * count], rest[-3:]
    copies = []
    for n, s in enumerate(states):
        givens = [received_refs[n][:, legs * first : legs * (first + length)] for first, length in parts]
        results = absorb(legs, width, givens, *ready_refs[3 * n : 3 * n + 3], proj_refs, comb_refs)
        squares = jnp.zeros((1, width), jnp.float32)
        for o, result in enumerate(results):
            sum_ref[o] = result
            squares = squares + jnp.sum(result * result, axis=0, keepdims=True)
        mean = jnp.sum(squares, axis=1, keepdims=True) * (1.0 / (legs * width * width))
        scale = lax.rsqrt(mean + eps)
        for o in range(legs):
            final_ref[n, :, o * width : (o + 1) * width] = (sum_ref[o] * scale).astype(jnp.bfloat16)
        copies.append(pltpu.make_async_copy(final_ref.at[n], out_ref.at[s, 0, 0], sems.at[n]))
        copies[-1].start()
    for copy in copies:
        copy.wait()


def local(
    boundary_in,
    site_tensors,
    spin_config,
    leg_charges,
    bond_charges,
    left_proj,
    right_proj,
    proj_ranks,
):
    states, width, legs = boundary_in.shape[0], boundary_in.shape[3], site_tensors.shape[4]
    every = list(range(states))
    squared, long = legs * legs, legs * width
    size = squared * GROUP
    vmem = pl.BlockSpec(memory_space=pltpu.VMEM)
    hbm = pl.BlockSpec(memory_space=pltpu.HBM)
    bf16, i32 = jnp.bfloat16, jnp.int32

    edge = jnp.concatenate([bond_charges, proj_ranks], axis=3)
    from_left = passed_along(edge, "col", 1)

    ready_shapes = [((long, width), bf16), ((size, size), bf16), ((long, width), bf16)]
    given_shapes = [((states, width, long), bf16), (bond_charges.shape, i32), ((states, 8, LANES), i32)]
    prepare_scratch = [
        pltpu.SMEM((1, 1, states), i32),
        pltpu.SMEM(leg_charges.shape, i32),
        pltpu.SMEM(proj_ranks.shape, i32),
        pltpu.VMEM(site_tensors.shape, bf16),
        pltpu.VMEM((states, width, long), bf16),
        pltpu.VMEM((states, width, long), bf16),
        pltpu.VMEM((LANES, LANES), jnp.float32),
        pltpu.VMEM((LANES, LANES), jnp.float32),
        pltpu.SemaphoreType.DMA((4 + 2 * states,)),
    ]
    given_scratch = [pltpu.VMEM((width, legs * length), bf16) for _, length in parts_of(width)]
    absorb_scratch = [pltpu.VMEM((long, legs * length), bf16) for _, length in parts_of(width)] * 2
    flops = 2 * (2 * width * long * long + long * long * GROUP)

    def call(kernel, name, out_shapes, in_specs, scratch, out_specs, **options):
        return pl.pallas_call(
            kernel,
            out_shape=[jax.ShapeDtypeStruct(*shape) for shape in out_shapes],
            in_specs=in_specs,
            out_specs=out_specs,
            scratch_shapes=scratch,
            compiler_params=pltpu.CompilerParams(vmem_limit_bytes=VMEM_BYTES),
            cost_estimate=pl.CostEstimate(flops=flops, bytes_accessed=8 * width * long, transcendentals=0),
            name=name,
            **options,
        )

    spins = jnp.transpose(spin_config, (1, 2, 0))
    spins, leg_charges, proj_ranks, site_tensors, bond_charges, boundary_in, left_proj, right_proj = (
        pltpu.with_memory_space_constraint(value, pltpu.HBM)
        for value in (spins, leg_charges, proj_ranks, site_tensors, bond_charges, boundary_in, left_proj, right_proj)
    )
    small = (spins, leg_charges, proj_ranks, site_tensors)
    bind = functools.partial
    given, charges, incoming, *ready = call(
        bind(prepare_first_kernel, every, legs, width), "prepare_first", given_shapes + ready_shapes * states,
        [hbm] * 8, prepare_scratch + [pltpu.SemaphoreType.DMA((1 + states,))], [vmem] * (3 + 3 * states),
    )(*small, bond_charges, boundary_in, left_proj, right_proj)
    halves = list(call(
        bind(first_kernel, every, legs, width), "first_absorption", [((width, long), bf16)] * states,
        [vmem] * (4 + 3 * states), given_scratch + absorb_scratch, [vmem] * states,
    )(from_left, given, charges, incoming, *ready))
    for s in every[1:]:
        halves[s : s + 1] = call(
            bind(rest_kernel, s, legs, width), "first_absorption_rest", [((width, long), bf16)],
            [vmem] * 5 + [hbm] * 7,
            [pltpu.VMEM(*shape) for shape in given_shapes[:1] + ready_shapes]
            + [pltpu.SemaphoreType.DMA] + given_scratch + absorb_scratch + prepare_scratch, [vmem],
        )(from_left, charges, incoming, halves[s], halves[s - 1], *small, boundary_in, left_proj, right_proj)
    last = halves[-1]
    received = [swapped(half, "row", 0) for half in halves]
    ready = call(
        bind(prepare_second_kernel, every, legs, width), "prepare_second", ready_shapes * states,
        [vmem] * 2 + [hbm] * 6, prepare_scratch, [vmem] * (3 * states),
    )(from_left, last, *small, left_proj, right_proj)
    out = None
    for group in [[s] for s in every]:
        more = [] if out is None else [out]
        (out,) = call(
            bind(second_kernel, group, legs, width), "second_absorption", [(boundary_in.shape, bf16)],
            [vmem] * (4 * len(group)) + [hbm] * len(more),
            absorb_scratch
            + [
                pltpu.VMEM((legs, width, width), jnp.float32),
                pltpu.VMEM((len(group), width, long), bf16),
                pltpu.SemaphoreType.DMA((len(group),)),
            ],
            [hbm], input_output_aliases={4 * len(group): 0} if more else {},
        )(*[received[s] for s in group], *ready[3 * group[0] : 3 * group[-1] + 3], *more)
    return out


def solution(mesh):
    placed = (
        P(None, "row", "col", None, None),
        P(None, "row", "col", None, None, None, None, None),
        P(None, "row", "col"),
        P(None, "row", "col", None, None),
        P(None, "row", "col", None),
        P(None, "row", "col", None, None, None),
        P(None, "row", "col", None, None, None),
        P(None, "row", "col", None),
    )
    return jax.shard_map(
        local,
        mesh=mesh,
        in_specs=placed,
        out_specs=P(None, "row", "col", None, None),
        check_vma=False,
    )
```

```python
import functools

import jax
import jax.numpy as jnp
from jax import lax
from jax.experimental import pallas as pl
from jax.experimental.pallas import tpu as pltpu
from jax.sharding import PartitionSpec as P

eps = 1e-06
VMEM_BYTES = 32 * 1024 * 1024
GROUP = 16
LANES = 128


def passed_along(value, axis, steps):
    count = lax.axis_size(axis)
    pairs = [(source, (source + steps) % count) for source in range(count)]
    return lax.ppermute(value, axis, pairs)


def swapped(value, axis, distance):
    mask = 2**distance
    pairs = [(source, source ^ mask) for source in range(lax.axis_size(axis))]
    return lax.ppermute(value, axis, pairs)


def pick(index, values):
    out = jnp.zeros_like(index)
    for j, value in enumerate(values):
        out = jnp.where(index == j, value, out)
    return out


def expand_block(s, legs, natural, site_ref, spin_ref, leg_ref, by_left_ref, by_right_ref, kron_ref):
    squared = legs * legs
    spin = spin_ref[0, 0, s]
    leg = [[leg_ref[s, 0, 0, j, t] for t in range(legs)] for j in range(4)]
    for l in range(legs):
        for e in range(legs):
            tile = jnp.where(spin == 1, site_ref[s, 0, 0, 1, l, e], site_ref[s, 0, 0, 0, l, e])
            tile = tile.astype(jnp.float32)
            by_left_ref[l * legs : (l + 1) * legs, e * legs : (e + 1) * legs] = tile
            by_right_ref[e * legs : (e + 1) * legs, l * legs : (l + 1) * legs] = tile
    turned = jnp.transpose(by_left_ref[...])[:squared, :squared]
    entries = jnp.where(natural, turned, by_right_ref[:squared, :squared])
    row = lax.broadcasted_iota(jnp.int32, (squared, squared), 0)
    col = lax.broadcasted_iota(jnp.int32, (squared, squared), 1)
    right, outer, left, inner = row // legs, row % legs, col // legs, col % legs
    up, down = jnp.where(natural, inner, outer), jnp.where(natural, outer, inner)
    balance = spin + pick(left, leg[0]) + pick(up, leg[2]) - pick(right, leg[1]) - pick(down, leg[3])
    entries = jnp.where(balance == 0, entries, 0.0).astype(jnp.bfloat16)
    size = squared * GROUP
    tall = lax.broadcasted_iota(jnp.int32, (size, squared), 0) // GROUP
    tall = (tall == lax.broadcasted_iota(jnp.int32, (size, squared), 1)).astype(jnp.bfloat16)
    wide = lax.broadcasted_iota(jnp.int32, (squared, size), 1) // GROUP
    wide = (wide == lax.broadcasted_iota(jnp.int32, (squared, size), 0)).astype(jnp.bfloat16)
    spread = jnp.dot(tall, entries, preferred_element_type=jnp.float32).astype(jnp.bfloat16)
    spread = jnp.dot(spread, wide, preferred_element_type=jnp.float32)
    row = lax.broadcasted_iota(jnp.int32, (size, size), 0)
    col = lax.broadcasted_iota(jnp.int32, (size, size), 1)
    kron_ref[...] = jnp.where(row % GROUP == col % GROUP, spread, 0.0).astype(jnp.bfloat16)


def stack_left(legs, width, rank, left_ref, stack_ref):
    for l in range(legs):
        part = left_ref[:, l * width : (l + 1) * width]
        if rank is not None:
            kept = lax.broadcasted_iota(jnp.int32, (width, 1), 0) < rank
            part = jnp.where(kept, part, jnp.zeros_like(part))
        stack_ref[l * width : (l + 1) * width, :] = part


def parts_of(width):
    return [(first, min(LANES, width - first)) for first in range(0, width, LANES)]


def turn_right(legs, width, rank, right_ref, turned_ref):
    kept = lax.broadcasted_iota(jnp.int32, (width, width), 1) < rank
    for e in range(legs):
        turned = jnp.transpose(right_ref[:, e * width : (e + 1) * width])
        turned = jnp.where(kept, turned, jnp.zeros_like(turned))
        for first, length in parts_of(width):
            at = legs * first + e * length
            turned_ref[at : at + length, :] = turned[first : first + length, :]


def project(legs, width, given, stack_ref, proj_ref):
    for l in range(legs):
        rows = slice(l * width, (l + 1) * width)
        proj = jnp.dot(stack_ref[rows, :], given, preferred_element_type=jnp.float32)
        proj_ref[rows, :] = proj.astype(jnp.bfloat16)


def combine(legs, width, length, kron_ref, proj_ref, comb_ref):
    side = 2 * LANES // length
    for q in range(0, width, side * GROUP):
        places = [q + h * GROUP for h in range(side)]
        part = jnp.concatenate(
            [
                jnp.concatenate(
                    [
                        proj_ref[l * width + k : l * width + k + GROUP, i * length : (i + 1) * length]
                        for k in places
                    ],
                    axis=1,
                )
                for l in range(legs)
                for i in range(legs)
            ],
            axis=0,
        )
        comb = jnp.dot(kron_ref[...], part, preferred_element_type=jnp.float32).astype(jnp.bfloat16)
        for o in range(legs):
            for h, k in enumerate(places):
                comb_ref[o * width + k : o * width + k + GROUP, :] = jnp.concatenate(
                    [
                        comb[(e * legs + o) * GROUP : (e * legs + o + 1) * GROUP, h * length : (h + 1) * length]
                        for e in range(legs)
                    ],
                    axis=1,
                )


def absorb(legs, width, givens, stack_ref, kron_ref, turned_ref, proj_refs, comb_refs, parts=None):
    parts = parts or parts_of(width)
    for given, proj_ref in zip(givens, proj_refs):
        project(legs, width, given, stack_ref, proj_ref)
    for (_, length), proj_ref, comb_ref in zip(parts, proj_refs, comb_refs):
        combine(legs, width, length, kron_ref, proj_ref, comb_ref)
    results = []
    for o in range(legs):
        result = None
        for (first, length), comb_ref in zip(parts, comb_refs):
            term = jnp.dot(
                comb_ref[o * width : (o + 1) * width, :],
                turned_ref[legs * first : legs * (first + length), :],
                preferred_element_type=jnp.float32,
            )
            result = term if result is None else result + term
        results.append(result)
    return results


def prepare(
    states, step, legs, width, natural, rank_left, fetch_small,
    spin_in, leg_in, rank_in, site_in, left_in, right_in, ready_refs,
    spin_ref, leg_ref, rank_ref, site_ref, left_ref, right_ref, by_left_ref, by_right_ref, sems,
):
    copies = [
        pltpu.make_async_copy(source.at[s, 0, 0, step], target.at[s], sems.at[4 + 2 * s + j])
        for s in states
        for j, (source, target) in enumerate([(right_in, right_ref), (left_in, left_ref)])
    ]
    if fetch_small:
        copies += [
            pltpu.make_async_copy(source, target, sems.at[j])
            for j, (source, target) in enumerate(
                [(spin_in, spin_ref), (leg_in, leg_ref), (rank_in, rank_ref), (site_in, site_ref)]
            )
        ]
    for copy in copies:
        copy.start()
    for copy in copies:
        copy.wait()
    for n, s in enumerate(states):
        stack_ref, kron_ref, turned_ref = ready_refs[3 * n : 3 * n + 3]
        expand_block(s, legs, natural, site_ref, spin_ref, leg_ref, by_left_ref, by_right_ref, kron_ref)
        turn_right(legs, width, rank_ref[s, 0, 0, step], right_ref.at[s], turned_ref)
        stack_left(legs, width, None if rank_left is None else rank_left(s), left_ref.at[s], stack_ref)


def rank_of(s, step, width, from_left_ref):
    return from_left_ref[s, 0, :, width + step : width + step + 1]


def is_top_first():
    return lax.rem(lax.axis_index("row"), 2) == 0


def prepare_first_kernel(states, legs, width, *rest):
    spin_in, leg_in, rank_in, site_in, charge_in, given_in, left_in, right_in = rest[:8]
    given_ref, charge_ref, incoming_ref, *rest = rest[8:]
    ready_refs, scratch, more = rest[: 3 * len(states)], rest[3 * len(states) : -1], rest[-1]
    sources = (spin_in, leg_in, rank_in, site_in, left_in, right_in)
    top_first = is_top_first()
    copies = [
        pltpu.make_async_copy(given_in.at[0, 0, 0], given_ref.at[0], more.at[0]),
        pltpu.make_async_copy(charge_in, charge_ref, more.at[1]),
    ]
    for copy in copies:
        copy.start()
    prepare(states[:1], 0, legs, width, top_first, None, True, *sources, ready_refs[:3], *scratch)
    leg_ref = scratch[1]
    for s in states:
        for i in range(legs):
            incoming = jnp.where(top_first, leg_ref[s, 0, 0, 2, i], leg_ref[s, 0, 0, 3, i])
            incoming_ref[s, i : i + 1, :] = jnp.full((1, LANES), incoming, jnp.int32)
    for copy in copies:
        copy.wait()

    @pl.when(top_first)
    def _():
        fetches = [pltpu.make_async_copy(given_in.at[s, 0, 0], given_ref.at[s], more.at[s + 1]) for s in states[1:]]
        for fetch in fetches:
            fetch.start()
        prepare(states[1:], 0, legs, width, top_first, None, False, *sources, ready_refs[3:], *scratch)
        for fetch in fetches:
            fetch.wait()


def prepare_second_kernel(states, legs, width, from_left_ref, _after, *rest):
    prepare(
        states, 1, legs, width, jnp.logical_not(is_top_first()), lambda s: rank_of(s, 1, width, from_left_ref), True,
        *rest[:6], rest[6 : 6 + 3 * len(states)], *rest[6 + 3 * len(states) :],
    )


def absorb_first(
    s, legs, width, from_left_ref, given_ref, charge_ref, incoming_ref, ready_refs, half_ref, scratch
):
    parts = parts_of(width)
    count = len(parts)
    given_refs, proj_refs, comb_refs = scratch[:count], scratch[count : 2 * count], scratch[2 * count :]
    row_charge = from_left_ref[s, 0, :, :width].astype(jnp.float32)
    left_charge = jnp.transpose(jnp.broadcast_to(row_charge, (LANES, width)))[:, :1]
    right_charge = charge_ref[s, 0].astype(jnp.float32)
    wanted = [right_charge - incoming_ref[s, i : i + 1, :1].astype(jnp.float32) for i in range(legs)]
    given = given_ref[s]
    given = jnp.where(left_charge == jnp.concatenate(wanted, axis=1), given, jnp.zeros_like(given))
    for part_ref, (first, length) in zip(given_refs, parts):
        for i in range(legs):
            at = i * width + first
            part_ref[:, i * length : (i + 1) * length] = given[:, at : at + length]
    givens = [part_ref[...] for part_ref in given_refs]
    results = absorb(legs, width, givens, *ready_refs, proj_refs, comb_refs)
    kept = lax.broadcasted_iota(jnp.int32, (width, 1), 0) < rank_of(s, 0, width, from_left_ref)
    for first, length in parts:
        for o, result in enumerate(results):
            part = jnp.where(kept, result[:, first : first + length], 0.0)
            if isinstance(half_ref, tuple):
                target_ref, at = half_ref[parts.index((first, length))], o * length
            else:
                target_ref, at = half_ref, legs * first + o * length
            target_ref[:, at : at + length] = part.astype(jnp.bfloat16)


def first_kernel(states, legs, width, from_left_ref, given_ref, charge_ref, incoming_ref, *rest):
    count = len(states)
    ready_refs, half_refs, scratch = rest[: 3 * count], rest[3 * count : 4 * count], rest[4 * count :]
    edges = (from_left_ref, given_ref, charge_ref, incoming_ref)
    absorb_first(0, legs, width, *edges, ready_refs[:3], half_refs[0], scratch)

    @pl.when(is_top_first())
    def _():
        for s in states[1:]:
            absorb_first(s, legs, width, *edges, ready_refs[3 * s : 3 * s + 3], half_refs[s], scratch)


def rest_kernel(s, legs, width, from_left_ref, charge_ref, incoming_ref, half_in_ref, _after, *rest):
    parts = parts_of(width)
    spin_in, leg_in, rank_in, site_in, given_in, left_in, right_in = rest[:7]
    half_refs, given_ref, rest = tuple(rest[7 : 7 + len(parts)]), rest[7 + len(parts)], rest[8 + len(parts) :]
    ready_refs, sem, rest = rest[:3], rest[3], rest[4:]
    scratch, more = rest[: 3 * len(parts_of(width))], rest[3 * len(parts_of(width)) :]
    top_first = is_top_first()

    @pl.when(top_first)
    def _():
        for half_ref, (first, length) in zip(half_refs, parts):
            half_ref[...] = half_in_ref[:, legs * first : legs * (first + length)]

    @pl.when(jnp.logical_not(top_first))
    def _():
        fetch = pltpu.make_async_copy(given_in.at[s, 0, 0], given_ref.at[s], sem)
        fetch.start()
        prepare(
            [s], 0, legs, width, top_first, None, True,
            spin_in, leg_in, rank_in, site_in, left_in, right_in, ready_refs, *more,
        )
        fetch.wait()
        absorb_first(
            s, legs, width, from_left_ref, given_ref, charge_ref, incoming_ref, ready_refs, half_refs, scratch
        )


def second_kernel(states, legs, width, *rest):
    parts = parts_of(width)
    count = len(parts)
    received_refs, ready_refs = rest[: len(states)], rest[len(states) : 4 * len(states)]
    proj_refs, comb_refs = rest[-3 - 2 * count : -3 - count], rest[-3 - count : -3]
    out_ref, (sum_ref, final_ref, sems) = rest[-4 - 2 * count], rest[-3:]
    copies = []
    for n, s in enumerate(states):
        givens = [received_refs[n][:, legs * first : legs * (first + length)] for first, length in parts]
        results = absorb(legs, width, givens, *ready_refs[3 * n : 3 * n + 3], proj_refs, comb_refs)
        squares = jnp.zeros((1, width), jnp.float32)
        for o, result in enumerate(results):
            sum_ref[o] = result
            squares = squares + jnp.sum(result * result, axis=0, keepdims=True)
        mean = jnp.sum(squares, axis=1, keepdims=True) * (1.0 / (legs * width * width))
        scale = lax.rsqrt(mean + eps)
        for o in range(legs):
            final_ref[n, :, o * width : (o + 1) * width] = (sum_ref[o] * scale).astype(jnp.bfloat16)
        copies.append(pltpu.make_async_copy(final_ref.at[n], out_ref.at[s, 0, 0], sems.at[n]))
        copies[-1].start()
    for copy in copies:
        copy.wait()


def second_part_kernel(p, legs, width, received_ref, *rest):
    *rest, total_ref, proj_ref, comb_ref = rest
    before = rest[4:]
    results = absorb(
        legs, width, [received_ref[...]], *rest[:3], [proj_ref], [comb_ref], parts_of(width)[p : p + 1]
    )
    for o, result in enumerate(results):
        total_ref[o] = before[0][o] + result if before else result


def second_last_kernel(s, p, legs, width, received_ref, stack_ref, kron_ref, turned_ref, total_ref, _out, *rest):
    out_ref, proj_ref, comb_ref, sum_ref, final_ref, sem = rest
    ready_refs = (stack_ref, kron_ref, turned_ref)
    results = absorb(legs, width, [received_ref[...]], *ready_refs, [proj_ref], [comb_ref], parts_of(width)[p : p + 1])
    squares = jnp.zeros((1, width), jnp.float32)
    for o, result in enumerate(results):
        result = total_ref[o] + result
        sum_ref[o] = result
        squares = squares + jnp.sum(result * result, axis=0, keepdims=True)
    mean = jnp.sum(squares, axis=1, keepdims=True) * (1.0 / (legs * width * width))
    scale = lax.rsqrt(mean + eps)
    for o in range(legs):
        final_ref[:, o * width : (o + 1) * width] = (sum_ref[o] * scale).astype(jnp.bfloat16)
    copy = pltpu.make_async_copy(final_ref, out_ref.at[s, 0, 0], sem)
    copy.start()
    copy.wait()


def local(
    boundary_in,
    site_tensors,
    spin_config,
    leg_charges,
    bond_charges,
    left_proj,
    right_proj,
    proj_ranks,
):
    states, width, legs = boundary_in.shape[0], boundary_in.shape[3], site_tensors.shape[4]
    every = list(range(states))
    squared, long = legs * legs, legs * width
    size = squared * GROUP
    vmem = pl.BlockSpec(memory_space=pltpu.VMEM)
    hbm = pl.BlockSpec(memory_space=pltpu.HBM)
    bf16, i32 = jnp.bfloat16, jnp.int32

    edge = jnp.concatenate([bond_charges, proj_ranks], axis=3)
    from_left = passed_along(edge, "col", 1)

    ready_shapes = [((long, width), bf16), ((size, size), bf16), ((long, width), bf16)]
    given_shapes = [((states, width, long), bf16), (bond_charges.shape, i32), ((states, 8, LANES), i32)]
    prepare_scratch = [
        pltpu.SMEM((1, 1, states), i32),
        pltpu.SMEM(leg_charges.shape, i32),
        pltpu.SMEM(proj_ranks.shape, i32),
        pltpu.VMEM(site_tensors.shape, bf16),
        pltpu.VMEM((states, width, long), bf16),
        pltpu.VMEM((states, width, long), bf16),
        pltpu.VMEM((LANES, LANES), jnp.float32),
        pltpu.VMEM((LANES, LANES), jnp.float32),
        pltpu.SemaphoreType.DMA((4 + 2 * states,)),
    ]
    given_scratch = [pltpu.VMEM((width, legs * length), bf16) for _, length in parts_of(width)]
    absorb_scratch = [pltpu.VMEM((long, legs * length), bf16) for _, length in parts_of(width)] * 2
    flops = 2 * (2 * width * long * long + long * long * GROUP)

    def call(kernel, name, out_shapes, in_specs, scratch, out_specs, **options):
        return pl.pallas_call(
            kernel,
            out_shape=[jax.ShapeDtypeStruct(*shape) for shape in out_shapes],
            in_specs=in_specs,
            out_specs=out_specs,
            scratch_shapes=scratch,
            compiler_params=pltpu.CompilerParams(vmem_limit_bytes=VMEM_BYTES),
            cost_estimate=pl.CostEstimate(flops=flops, bytes_accessed=8 * width * long, transcendentals=0),
            name=name,
            **options,
        )

    spins = jnp.transpose(spin_config, (1, 2, 0))
    spins, leg_charges, proj_ranks, site_tensors, bond_charges, boundary_in, left_proj, right_proj = (
        pltpu.with_memory_space_constraint(value, pltpu.HBM)
        for value in (spins, leg_charges, proj_ranks, site_tensors, bond_charges, boundary_in, left_proj, right_proj)
    )
    small = (spins, leg_charges, proj_ranks, site_tensors)
    bind = functools.partial
    given, charges, incoming, *ready = call(
        bind(prepare_first_kernel, every, legs, width), "prepare_first", given_shapes + ready_shapes * states,
        [hbm] * 8, prepare_scratch + [pltpu.SemaphoreType.DMA((1 + states,))], [vmem] * (3 + 3 * states),
    )(*small, bond_charges, boundary_in, left_proj, right_proj)
    halves = list(call(
        bind(first_kernel, every, legs, width), "first_absorption", [((width, long), bf16)] * states,
        [vmem] * (4 + 3 * states), given_scratch + absorb_scratch, [vmem] * states,
    )(from_left, given, charges, incoming, *ready))
    s = states - 1
    split = call(
        bind(rest_kernel, s, legs, width), "first_absorption_rest",
        [((width, legs * length), bf16) for _, length in parts_of(width)], [vmem] * 5 + [hbm] * 7,
        [pltpu.VMEM(*shape) for shape in given_shapes[:1] + ready_shapes]
        + [pltpu.SemaphoreType.DMA] + given_scratch + absorb_scratch + prepare_scratch, [vmem] * len(parts_of(width)),
    )(from_left, charges, incoming, halves[s], halves[s - 1], *small, boundary_in, left_proj, right_proj)
    last = split[0]
    ready = call(
        bind(prepare_second_kernel, every, legs, width), "prepare_second", ready_shapes * states,
        [vmem] * 2 + [hbm] * 6, prepare_scratch, [vmem] * (3 * states),
    )(from_left, last, *small, left_proj, right_proj)
    *others, tail = split
    tail, ready = lax.optimization_barrier((tail, ready))
    received = [swapped(half, "row", 0) for half in halves[:-1]]
    last_received = [swapped(part, "row", 0) for part in (*others, tail)]
    out = None
    for group in [[s] for s in every[:-1]]:
        more = [] if out is None else [out]
        (out,) = call(
            bind(second_kernel, group, legs, width), "second_absorption", [(boundary_in.shape, bf16)],
            [vmem] * (4 * len(group)) + [hbm] * len(more),
            absorb_scratch
            + [
                pltpu.VMEM((legs, width, width), jnp.float32),
                pltpu.VMEM((len(group), width, long), bf16),
                pltpu.SemaphoreType.DMA((len(group),)),
            ],
            [hbm], input_output_aliases={4 * len(group): 0} if more else {},
        )(*[received[s] for s in group], *ready[3 * group[0] : 3 * group[-1] + 3], *more)
    out = pltpu.with_memory_space_constraint(out, pltpu.HBM)
    own, total = ready[-3:], []
    for p, (_, length) in enumerate(parts_of(width)[:-1]):
        total = call(
            bind(second_part_kernel, p, legs, width), "second_absorption_part", [((legs, width, width), jnp.float32)],
            [vmem] * 4 + [hbm] + [vmem] * len(total), [pltpu.VMEM((long, legs * length), bf16)] * 2, [vmem],
        )(last_received[p], *own, out, *total)
    length = parts_of(width)[-1][1]
    (out,) = call(
        bind(second_last_kernel, states - 1, len(parts_of(width)) - 1, legs, width), "second_absorption_last",
        [(boundary_in.shape, bf16)], [vmem] * 5 + [hbm],
        [pltpu.VMEM((long, legs * length), bf16)] * 2
        + [pltpu.VMEM((legs, width, width), jnp.float32), pltpu.VMEM((width, long), bf16), pltpu.SemaphoreType.DMA],
        [hbm], input_output_aliases={5: 0},
    )(last_received[-1], *own, *total, out)
    return out


def solution(mesh):
    placed = (
        P(None, "row", "col", None, None),
        P(None, "row", "col", None, None, None, None, None),
        P(None, "row", "col"),
        P(None, "row", "col", None, None),
        P(None, "row", "col", None),
        P(None, "row", "col", None, None, None),
        P(None, "row", "col", None, None, None),
        P(None, "row", "col", None),
    )
    return jax.shard_map(
        local,
        mesh=mesh,
        in_specs=placed,
        out_specs=P(None, "row", "col", None, None),
        check_vma=False,
    )
```
